128 devices in a mesh: dp: 4 (over y_hi, core), seq: 32 (over y_lo, x, z).
Axes of the slice: x: 4, y: 4 (y_hi: 2, y_lo: 2; y = y_hi * 2 + y_lo), z: 4, core: 2. Of those that a mesh axis runs over, the one named last changes fastest.
Arguments:
- tokens: bfloat16 [4, 4096, 1024], P('dp', 'seq'), may hold values from -6 to 6
- out_grad: bfloat16 [4, 4096, 1024], P('dp', 'seq'), may hold values from -6 to 6
- piece_starts: int32 [4, 6], P('dp'), may hold values from 0 to 3840, as said below
- span_order: int32 [4, 64], P('dp'), may hold values from 0 to 63, each once within a row
- ln1_gain: bfloat16 [1, 1024], P(None, ('dp', 'seq')), may hold values from 0.5 to 1.5
- ln1_bias: bfloat16 [1, 1024], P(None, ('dp', 'seq')), may hold values from -4 to 4
- qkv_weight: bfloat16 [1, 1024, 3072], P(None, ('dp', 'seq')), may hold values from -0.1875 to 0.1875
- query_bias: bfloat16 [1, 1024], P(None, ('dp', 'seq')), may hold values from -4 to 4
- value_bias: bfloat16 [1, 1024], P(None, ('dp', 'seq')), may hold values from -4 to 4
- out_weight: bfloat16 [1, 1024, 1024], P(None, ('dp', 'seq')), may hold values from -2 to 2
- out_bias: bfloat16 [1, 1024], P(None, ('dp', 'seq')), may hold values from -3 to 3
- ln2_gain: bfloat16 [1, 1024], P(None, ('dp', 'seq')), may hold values from 0.5 to 1.5
- ln2_bias: bfloat16 [1, 1024], P(None, ('dp', 'seq')), may hold values from -4 to 4
- fc_weight: bfloat16 [1, 1024, 4096], P(None, ('dp', 'seq')), may hold values from -0.1875 to 0.1875
- fc_bias: bfloat16 [1, 4096], P(None, ('dp', 'seq')), may hold values from -4 to 4
- proj_weight: bfloat16 [1, 4096, 1024], P(None, ('dp', 'seq')), may hold values from -0.09375 to 0.09375
- proj_bias: bfloat16 [1, 1024], P(None, ('dp', 'seq')), may hold values from -3 to 3
Outputs:
- out: bfloat16 [4, 4096, 1024], P('dp', 'seq')
- grad_tokens: float32 [4, 4096, 1024], P('dp', 'seq')
- grad_ln1_gain: float32 [1, 1024], P(None, ('dp', 'seq'))
- grad_ln1_bias: float32 [1, 1024], P(None, ('dp', 'seq'))
- grad_qkv_weight: float32 [1, 1024, 3072], P(None, ('dp', 'seq'))
- grad_query_bias: float32 [1, 1024], P(None, ('dp', 'seq'))
- grad_value_bias: float32 [1, 1024], P(None, ('dp', 'seq'))
- grad_out_weight: float32 [1, 1024, 1024], P(None, ('dp', 'seq'))
- grad_out_bias: float32 [1, 1024], P(None, ('dp', 'seq'))
- grad_ln2_gain: float32 [1, 1024], P(None, ('dp', 'seq'))
- grad_ln2_bias: float32 [1, 1024], P(None, ('dp', 'seq'))
- grad_fc_weight: float32 [1, 1024, 4096], P(None, ('dp', 'seq'))
- grad_fc_bias: float32 [1, 4096], P(None, ('dp', 'seq'))
- grad_proj_weight: float32 [1, 4096, 1024], P(None, ('dp', 'seq'))
- grad_proj_bias: float32 [1, 1024], P(None, ('dp', 'seq'))
The draws below stay inside these ranges and needn't reach their ends.
Inputs may be any that keep to these rules, and one draw needn't show every extreme that they name: `piece_starts`: in each row the starts rise, and each start is at least 256 after the one before, so pieces never intersect. `span_order`: each row names every block 0 to 63 exactly once.
All inputs are finite; a program needn't handle non-finite values.
Results may differ from the reference program's by a relative error of at most 0.0158.
Values may be sent and summed in bfloat16 or wider, within the bound.
No kernel may reach another device: no remote copies, remote signals or barrier semaphores. Data moves between devices by JAX's collectives and lax.ppermute only.
A program may use at most 192 MiB of HBM per device.

```python
import jax
import jax.numpy as jnp
from jax import lax

D = 1024
HEADS = 16
FF = 4096
HEAD_DIM = 64
LAYERS = 1
PIECE = 256
SPAN = 64
SPANS = 64
LENGTH = 4096
SEQS = 4
PIECES = 6


def draw_piece_starts(key, part):
    key = jax.random.fold_in(key, 7)
    spare = LENGTH - PIECES * PIECE
    offsets = jax.random.randint(key, (SEQS, PIECES), 0, spare + 1, dtype=jnp.int32)
    offsets = jnp.sort(offsets, axis=1)
    return (offsets + jnp.arange(PIECES, dtype=jnp.int32)[None, :] * PIECE).astype(jnp.int32)


def block_scale(stream_key, extent, split, low, largest):
    def one(dim, parts):
        steps = jax.random.uniform(jax.random.fold_in(jax.random.fold_in(stream_key, 6), dim), (parts,), jnp.float32, low / len(split), largest / len(split))
        return jnp.repeat(jnp.exp(steps), extent[dim] // parts).reshape((-1,) + (1,) * (len(extent) - dim - 1))

    level = one(*split[0])
    for cut in split[1:]:
        level = level * one(*cut)
    return level


def normal_values(stream_key, extent, width, reach, cuts=(), held_as=jnp.bfloat16):
    factor_of = block_scale(stream_key, extent, cuts, -0.22, 0.18) if cuts else 1.0
    entries = jax.random.normal(stream_key, extent, jnp.float32) * width * factor_of
    return jnp.minimum(jnp.maximum(entries, -reach), reach).astype(held_as)


def setup_inputs(seed: int = 0) -> dict:
    streams_of = jax.random.split(jax.random.key(seed), 18)
    tokens = normal_values(streams_of[0], (SEQS, LENGTH, D), 1.0, 6.0, ((0, 4), (1, 32)))
    out_grad = normal_values(streams_of[1], (SEQS, LENGTH, D), 1.0, 6.0, ((0, 4), (1, 32)))
    piece_starts = draw_piece_starts(jax.random.fold_in(streams_of[17], 71), 0)
    span_order = jax.vmap(lambda own: jax.random.permutation(own, SPANS))(jax.random.split(streams_of[3], SEQS)).reshape((SEQS, SPANS)).astype(jnp.int32)
    ln1_gain = jnp.clip(1.0 + 0.1 * jax.random.normal(streams_of[4], (LAYERS, D), jnp.float32), 0.5, 1.5).astype(jnp.bfloat16)
    ln1_bias = normal_values(streams_of[5], (LAYERS, D), 0.3, 4.0, ((1, 128),))
    qkv_weight = normal_values(streams_of[6], (LAYERS, D, 3 * D), D ** -0.5, 0.1875, ((1, 128),))
    query_bias = normal_values(streams_of[7], (LAYERS, D), 0.3, 4.0, ((1, 128),))
    value_bias = normal_values(streams_of[8], (LAYERS, D), 0.3, 4.0, ((1, 128),))
    out_weight = normal_values(streams_of[9], (LAYERS, D, D), (max(1, D * 32 // LENGTH)) ** -0.5, 2.0, ((1, 128),))
    out_bias = normal_values(streams_of[10], (LAYERS, D), 0.2, 3.0, ((1, 128),))
    ln2_gain = jnp.clip(1.0 + 0.1 * jax.random.normal(streams_of[11], (LAYERS, D), jnp.float32), 0.5, 1.5).astype(jnp.bfloat16)
    ln2_bias = normal_values(streams_of[12], (LAYERS, D), 0.3, 4.0, ((1, 128),))
    fc_weight = normal_values(streams_of[13], (LAYERS, D, FF), D ** -0.5, 0.1875, ((1, 128),))
    fc_bias = normal_values(streams_of[14], (LAYERS, FF), 0.3, 4.0, ((1, 128),))
    proj_weight = normal_values(streams_of[15], (LAYERS, FF, D), FF ** -0.5, 0.09375, ((1, 128),))
    proj_bias = normal_values(streams_of[16], (LAYERS, D), 0.2, 3.0, ((1, 128),))
    return dict(tokens=tokens, out_grad=out_grad, piece_starts=piece_starts, span_order=span_order, ln1_gain=ln1_gain, ln1_bias=ln1_bias, qkv_weight=qkv_weight, query_bias=query_bias, value_bias=value_bias, out_weight=out_weight, out_bias=out_bias, ln2_gain=ln2_gain, ln2_bias=ln2_bias, fc_weight=fc_weight, fc_bias=fc_bias, proj_weight=proj_weight, proj_bias=proj_bias)


@jax.custom_vjp
def low(v):
    return lax.optimization_barrier(v.astype(jnp.bfloat16)).astype(jnp.float32)

@jax.custom_vjp
def low_back(v):
    return v

def low_keep(v):
    return (low(v), None)

def low_pass(kept, grad):
    return (grad,)

def back_keep(v):
    return (v, None)

def back_low(kept, grad):
    return (low(grad),)
low.defvjp(low_keep, low_pass)
low_back.defvjp(back_keep, back_low)
EPS = 1e-05
NEG = -1e+30

def matmul(left_side, right_side):
    return jnp.dot(left_side, right_side, precision=lax.Precision.HIGHEST, preferred_element_type=jnp.float32)

def layer_norm(values, gain, shift):
    center = values - lax.optimization_barrier(jnp.mean(values, axis=-1, keepdims=True))
    spread = lax.optimization_barrier(jnp.mean(center * center, axis=-1, keepdims=True))
    return center * lax.rsqrt(spread + EPS) * gain + shift

def gelu_tanh(values):
    return 0.5 * values * (1.0 + jnp.tanh(0.7978845608028654 * (values + 0.044715 * values * values * values)))

def piece_number(positions, starts):
    inside = (positions[:, None] >= starts[None, :]) & (positions[:, None] < starts[None, :] + PIECE)
    labels = jnp.arange(starts.shape[0], dtype=jnp.int32)[None, :] + 1
    return lax.optimization_barrier(jnp.sum(jnp.where(inside, labels, 0), axis=1)).astype(jnp.int32)

def allowed_mask(positions, starts):
    pieces = piece_number(positions, starts)
    causal = positions[None, :] <= positions[:, None]
    shared = (pieces[:, None] == pieces[None, :]) & (pieces[:, None] > 0)
    return causal | shared

def split_heads(values):
    return values.reshape(values.shape[0], HEADS, HEAD_DIM).transpose(1, 0, 2)

def attend_sequence(sequence_items):
    query_rows, key_rows, value_rows, positions, starts = sequence_items
    allowed = allowed_mask(positions, starts)
    score_scale = HEAD_DIM ** (-0.5)

    def one_head(head_items):
        query_head, key_head, value_head = head_items
        scores = low_back(matmul(query_head, key_head.T) * score_scale)
        scores = jnp.where(allowed, scores, NEG)
        maxima = lax.optimization_barrier(jnp.max(scores, axis=-1, keepdims=True))
        raised = jnp.exp(scores - maxima)
        attn_weights = low(raised / lax.optimization_barrier(jnp.sum(raised, axis=-1, keepdims=True)))
        return matmul(attn_weights, value_head)
    mixture = lax.map(jax.checkpoint(one_head), (split_heads(query_rows), split_heads(key_rows), split_heads(value_rows)))
    return mixture.transpose(1, 0, 2).reshape(query_rows.shape[0], HEADS * HEAD_DIM)

def by_sequence(values):
    return values.reshape(SEQS, LENGTH, D)

def block(hidden, weights, positions, piece_starts):
    first_gain, first_shift, qkv_matrix, query_shift, value_shift, out_matrix, out_shift, second_gain, second_shift, fc_matrix, fc_shift, proj_matrix, proj_shift = weights
    normed = low(layer_norm(hidden, first_gain, first_shift))
    projected = matmul(normed, qkv_matrix)
    query_rows = low(low_back(projected[:, :D] + query_shift))
    key_rows = low(low_back(projected[:, D:2 * D]))
    value_rows = low(low_back(projected[:, 2 * D:] + value_shift))
    attended = lax.map(attend_sequence, (by_sequence(query_rows), by_sequence(key_rows), by_sequence(value_rows), positions, piece_starts))
    attended = low(low_back(attended.reshape(SEQS * LENGTH, D)))
    middle = hidden + low_back(matmul(attended, out_matrix) + out_shift)
    normed_two = low(layer_norm(middle, second_gain, second_shift))
    pre_act = low_back(matmul(normed_two, fc_matrix) + fc_shift)
    activated = low(gelu_tanh(pre_act))
    return middle + low_back(matmul(activated, proj_matrix) + proj_shift)

def reference(tokens, out_grad, piece_starts, span_order, ln1_gain, ln1_bias, qkv_weight, query_bias, value_bias, out_weight, out_bias, ln2_gain, ln2_bias, fc_weight, fc_bias, proj_weight, proj_bias):
    params = tuple((weight.astype(jnp.float32) for weight in (ln1_gain, ln1_bias, qkv_weight, query_bias, value_bias, out_weight, out_bias, ln2_gain, ln2_bias, fc_weight, fc_bias, proj_weight, proj_bias)))
    positions = (span_order[:, :, None] * SPAN + jnp.arange(SPAN, dtype=jnp.int32)[None, None, :]).reshape(SEQS, LENGTH).astype(jnp.int32)

    def forward(inputs, weights):
        hidden = inputs.reshape(SEQS * LENGTH, D)
        for layer_index in range(LAYERS):
            hidden = block(hidden, tuple((weight[layer_index] for weight in weights)), positions, piece_starts)
        return hidden
    result, pull_back = jax.vjp(forward, tokens.astype(jnp.float32), params)
    grad_in, grad_weights = pull_back(out_grad.astype(jnp.float32).reshape(SEQS * LENGTH, D))
    return (result.reshape(SEQS, LENGTH, D).astype(jnp.bfloat16), grad_in.reshape(SEQS, LENGTH, D), grad_weights[0], grad_weights[1], grad_weights[2], grad_weights[3], grad_weights[4], grad_weights[5], grad_weights[6], grad_weights[7], grad_weights[8], grad_weights[9], grad_weights[10], grad_weights[11], grad_weights[12])
```

```python
import functools

import jax
import jax.numpy as jnp
from jax import lax
from jax.experimental import pallas as pl
from jax.experimental.pallas import tpu as pltpu
from jax.sharding import Mesh, PartitionSpec as P

D = 1024
PIECE = 256
EPS = 1e-05
NEG = -1e30
LOG2E = 1.4426950408889634
BF = jnp.bfloat16
F32 = jnp.float32
AXES = ("yh", "core", "yl", "x", "z")
Y = ("yh", "yl")
QB = 256
KB = 512


def plain_product(left_side, right_side):
    return jnp.dot(left_side, right_side, preferred_element_type=F32)


def left_product(left_side, right_side):
    return lax.dot_general(
        left_side, right_side, (((0,), (0,)), ((), ())), preferred_element_type=F32
    )


def right_product(left_side, right_side):
    return lax.dot_general(
        left_side, right_side, (((1,), (1,)), ((), ())), preferred_element_type=F32
    )


def gelu_tanh(values):
    return (
        0.5
        * values
        * (1.0 + jnp.tanh(0.7978845608028654 * (values + 0.044715 * values * values * values)))
    )


def layer_norm(values, gain, shift):
    center = values - jnp.mean(values, axis=-1, keepdims=True)
    spread = jnp.mean(center * center, axis=-1, keepdims=True)
    return center * lax.rsqrt(spread + EPS) * gain + shift


def norm_backward(values, gain, grad):
    center = values - jnp.mean(values, axis=-1, keepdims=True)
    spread = jnp.mean(center * center, axis=-1, keepdims=True)
    scale = lax.rsqrt(spread + EPS)
    normed = center * scale
    pulled = grad * gain
    back = scale * (
        pulled
        - jnp.mean(pulled, axis=-1, keepdims=True)
        - normed * jnp.mean(pulled * normed, axis=-1, keepdims=True)
    )
    return back, normed


def shift(values, axis, step):
    return lax.ppermute(values, axis, [(i, (i + step) % 4) for i in range(4)])


def swap_core(values):
    return lax.ppermute(values, "core", [(0, 1), (1, 0)])


def ring_blocks(values, axis):
    return [values, shift(values, axis, -1), shift(values, axis, 2), shift(values, axis, 1)]


def ring_stack(values, axis):
    return jnp.stack(ring_blocks(values, axis))


def place_call(kernel, places, blocks, shapes):
    return pl.pallas_call(
        kernel,
        out_shape=[jax.ShapeDtypeStruct(shape, BF) for shape in shapes],
        in_specs=[pl.BlockSpec(memory_space=pltpu.SMEM)]
        + [pl.BlockSpec(memory_space=pltpu.VMEM)] * len(blocks),
        out_specs=[pl.BlockSpec(memory_space=pltpu.VMEM)] * len(shapes),
        compiler_params=pltpu.CompilerParams(vmem_limit_bytes=48 * 1024 * 1024),
    )(places, *blocks)


def around(place, step):
    return lax.rem(place + step, 4)


def feature_row(y, side, x):
    return pl.multiple_of((y // 2) * 512 + side * 256 + (y % 2) * 128 + x * 32, 32)


def place_first(places, *refs):
    sources, out = refs[:4], refs[4]
    for step in range(4):
        y = around(places[0], step)

        @pl.loop(0, 4)
        def _(turn):
            x = around(places[1], turn)
            for side in range(2):
                out[pl.ds(feature_row(y, side, x), 32), :] = sources[step][
                    turn, side * 32 : side * 32 + 32, :
                ]


def place_second(places, *refs):
    sources, fc, out = refs[:4], refs[4], refs[5]
    for step in range(4):
        z = around(places[2], step)
        columns = pl.ds(pl.multiple_of(z * 256, 256), 256)

        @pl.loop(0, 16)
        def _(turn):
            y, x = around(places[0], turn // 4), around(places[1], turn % 4)
            for side in range(2):
                fc[z, pl.ds(feature_row(y, side, x), 32), :] = sources[step][
                    turn // 4, turn % 4, side * 32 : side * 32 + 32, :
                ]
            row = pl.multiple_of((y * 4 + x) * 32, 32)
            block = sources[step][turn // 4, turn % 4, 64:80, :]
            out[pl.ds(row, 16), columns] = block[:, :256]
            out[pl.ds(row + 16, 16), columns] = block[:, 256:]


def place_third(places, *refs):
    sources, out = refs[:4], refs[4]
    for step in range(4):
        y = around(places[0], step)

        @pl.loop(0, 16)
        def _(turn):
            x, z = around(places[1], turn // 4), around(places[2], turn % 4)
            out[y, pl.ds(pl.multiple_of((x * 4 + z) * 32, 32), 32), :] = sources[step][
                turn // 4, turn % 4
            ]


def place_rows(places, own, other, out):
    for step in range(4):
        z = around(places[2], step)
        out[places[3], z] = own[step]
        out[1 - places[3], z] = other[step]


def ring_reduce(values, axis):
    place = lax.axis_index(axis)

    def block(step):
        return lax.dynamic_index_in_dim(values, (place + step) % 4, 0, keepdims=False)

    total = (
        block(0).astype(F32)
        + shift(block(1), axis, 1).astype(F32)
        + shift(block(2), axis, 2).astype(F32)
        + shift(block(3), axis, -1).astype(F32)
    )
    return total.astype(values.dtype)


def limit_of(position, starts):
    limit = position
    for start in starts:
        limit = jnp.where((position >= start) & (position < start + PIECE), start + PIECE - 1, limit)
    return limit


def lane_half(shape):
    return lax.broadcasted_iota(jnp.int32, shape, 1) < 64


def forward_kernel(
    order_ref, source_ref, where_ref, starts_ref, got_ref, kv_ref, q_ref, o_ref, lse_ref, msg_ref
):
    starts = [starts_ref[i] for i in range(6)]

    @pl.loop(0, 64)
    def _(span):
        stored = order_ref[span]
        kv_ref[pl.ds(pl.multiple_of(span * 64, 64), 64), :] = got_ref[
            stored // 8, pl.ds(pl.multiple_of((stored % 8) * 64, 64), 64), :
        ]

    @pl.loop(0, 32)
    def _(span):
        source = source_ref[span]
        packed = got_ref[
            source // 4, pl.ds(pl.multiple_of(512 + (source % 4) * 32, 32), 32), :
        ].astype(F32) * 0.125
        left = lane_half(packed.shape)
        row = pl.multiple_of(span * 64, 64)
        q_ref[pl.ds(row, 32), :] = jnp.where(left, packed, 0.0).astype(BF)
        q_ref[pl.ds(row + 32, 32), :] = jnp.where(left, pltpu.roll(packed, 64, 1), 0.0).astype(BF)

    @pl.loop(0, 2048 // QB)
    def _(block):
        row = pl.multiple_of(block * QB, QB)
        query = q_ref[pl.ds(row, QB), :]
        spans = QB // 64
        first = limit_of(where_ref[block * spans] * 64, starts)
        last = limit_of(where_ref[block * spans + spans - 1] * 64 + 63, starts)
        full = (first + 1) // KB
        count = last // KB + 1
        inner = lax.broadcasted_iota(jnp.int32, (64, 1), 0)
        position = jnp.concatenate(
            [where_ref[block * spans + i] * 64 + inner for i in range(spans)], axis=0
        )
        limit = limit_of(position, starts)

        def step(masked, index, carry):
            maxima, totals, mixture = carry
            begin = pl.multiple_of(index * KB, KB)
            pair = kv_ref[pl.ds(begin, KB), :]
            scores = right_product(query, pair)
            if masked:
                key_pos = begin + lax.broadcasted_iota(jnp.int32, (1, KB), 1)
                scores = jnp.where(key_pos <= limit, scores, NEG)
            higher = jnp.maximum(maxima, jnp.max(scores, axis=1, keepdims=True))
            raised = jnp.exp2((scores - higher) * LOG2E)
            fade = jnp.exp2((maxima - higher) * LOG2E)
            totals = totals * fade + jnp.sum(raised, axis=1, keepdims=True)
            mixture = mixture * fade + plain_product(raised.astype(BF), pair)
            return higher, totals, mixture

        carry = (
            jnp.full((QB, 1), NEG, F32),
            jnp.zeros((QB, 1), F32),
            jnp.zeros((QB, 128), F32),
        )
        carry = lax.fori_loop(0, full, functools.partial(step, False), carry)
        maxima, totals, mixture = lax.fori_loop(full, count, functools.partial(step, True), carry)
        attended = mixture / totals
        o_ref[pl.ds(row, QB), :] = attended.astype(BF)
        log_total = maxima * LOG2E + jnp.log2(totals)
        lse_ref[block] = jnp.transpose(jnp.broadcast_to(log_total, (QB, 128)))[0:8, :]
        turned = pltpu.roll(attended, 64, 1)
        for i in range(spans):
            top, bottom = turned[i * 64 : i * 64 + 32], attended[i * 64 + 32 : i * 64 + 64]
            msg_ref[source_ref[block * spans + i]] = jnp.where(
                lane_half(top.shape), top, bottom
            ).astype(BF)


def backward_kernel(
    order_ref,
    source_ref,
    where_ref,
    starts_ref,
    kv_ref,
    q_ref,
    o_ref,
    lse_ref,
    got_ref,
    msg_ref,
    do_ref,
    sum_ref,
):
    starts = [starts_ref[i] for i in range(6)]

    @pl.loop(0, 32)
    def _(span):
        packed = got_ref[source_ref[span]].astype(F32)
        left = lane_half(packed.shape)
        row = pl.multiple_of(span * 64, 64)
        do_ref[pl.ds(row, 32), :] = jnp.where(left, 0.0, pltpu.roll(packed, 64, 1)).astype(BF)
        do_ref[pl.ds(row + 32, 32), :] = jnp.where(left, 0.0, packed).astype(BF)

    sum_ref[...] = jnp.zeros_like(sum_ref)

    @pl.loop(0, 2048 // QB)
    def _(block):
        row = pl.multiple_of(block * QB, QB)
        query = q_ref[pl.ds(row, QB), :]
        grad = do_ref[pl.ds(row, QB), :]
        both = jnp.concatenate([query, grad], axis=0)
        spans = QB // 64
        first = limit_of(where_ref[block * spans] * 64, starts)
        last = limit_of(where_ref[block * spans + spans - 1] * 64 + 63, starts)
        full = (first + 1) // KB
        count = last // KB + 1
        inner = lax.broadcasted_iota(jnp.int32, (1, 64), 1)
        position = jnp.concatenate(
            [where_ref[block * spans + i] * 64 + inner for i in range(spans)], axis=1
        )
        limit = limit_of(position, starts)
        log_total = lse_ref[block][0:1, :]
        product = grad.astype(F32) * o_ref[pl.ds(row, QB), :].astype(F32)
        delta = lax.dot_general(
            jnp.ones((8, 128), F32),
            product,
            (((1,), (1,)), ((), ())),
            precision=lax.Precision.HIGHEST,
            preferred_element_type=F32,
        )[0:1, :]

        def step(masked, index, total):
            begin = pl.multiple_of(index * KB, KB)
            pair = kv_ref[pl.ds(begin, KB), :]
            scores = right_product(pair, query)
            if masked:
                key_pos = begin + lax.broadcasted_iota(jnp.int32, (KB, 1), 0)
                scores = jnp.where(key_pos <= limit, scores, NEG)
            weights = jnp.exp2(scores * LOG2E - log_total)
            grad_scores = (weights * (right_product(pair, grad) - delta)).astype(BF)
            sum_ref[pl.ds(begin, KB), :] += plain_product(
                jnp.concatenate([grad_scores, weights.astype(BF)], axis=1), both
            )
            return total + left_product(grad_scores, pair)

        total = jnp.zeros((QB, 128), F32)
        total = lax.fori_loop(0, full, functools.partial(step, False), total)
        total = lax.fori_loop(full, count, functools.partial(step, True), total) * 0.125
        turned = pltpu.roll(total, 64, 1)
        for i in range(spans):
            top, bottom = total[i * 64 : i * 64 + 32], turned[i * 64 + 32 : i * 64 + 64]
            source = source_ref[block * spans + i]
            msg_ref[
                source // 4, pl.ds(pl.multiple_of(512 + (source % 4) * 32, 32), 32), :
            ] = jnp.where(lane_half(top.shape), top, bottom).astype(BF)

    @pl.loop(0, 64)
    def _(span):
        stored = order_ref[span]
        msg_ref[stored // 8, pl.ds(pl.multiple_of((stored % 8) * 64, 64), 64), :] = sum_ref[
            pl.ds(pl.multiple_of(span * 64, 64), 64), :
        ].astype(BF)


def attend_forward(tables, got):
    shapes = [
        jax.ShapeDtypeStruct((4096, 128), BF),
        jax.ShapeDtypeStruct((2048, 128), BF),
        jax.ShapeDtypeStruct((2048, 128), BF),
        jax.ShapeDtypeStruct((2048 // QB, 8, QB), F32),
        jax.ShapeDtypeStruct((32, 32, 128), BF),
    ]
    return pl.pallas_call(
        forward_kernel,
        out_shape=shapes,
        in_specs=[pl.BlockSpec(memory_space=pltpu.SMEM)] * 4
        + [pl.BlockSpec(memory_space=pltpu.VMEM)],
        out_specs=[pl.BlockSpec(memory_space=pltpu.VMEM)] * 5,
        compiler_params=pltpu.CompilerParams(vmem_limit_bytes=48 * 1024 * 1024),
    )(*tables, got)


def attend_backward(tables, saved, got):
    return pl.pallas_call(
        backward_kernel,
        out_shape=jax.ShapeDtypeStruct((8, 640, 128), BF),
        in_specs=[pl.BlockSpec(memory_space=pltpu.SMEM)] * 4
        + [pl.BlockSpec(memory_space=pltpu.VMEM)] * 5,
        out_specs=pl.BlockSpec(memory_space=pltpu.VMEM),
        scratch_shapes=[pltpu.VMEM((2048, 128), BF), pltpu.VMEM((4096, 128), F32)],
        compiler_params=pltpu.CompilerParams(vmem_limit_bytes=48 * 1024 * 1024),
    )(*tables, *saved, got)


def order_tables(span_order, piece_starts, part):
    places = jnp.arange(64, dtype=jnp.int32)
    order = jnp.sum(jnp.where(span_order[None, :] == places[:, None], places[None, :], 0), axis=1)
    mine = lax.dynamic_index_in_dim(span_order.reshape(32, 2), part, 1, keepdims=False)
    rank = jnp.sum((mine[None, :] < mine[:, None]).astype(jnp.int32), axis=1)
    sources = jnp.arange(32, dtype=jnp.int32)
    hit = rank[None, :] == sources[:, None]
    source = jnp.sum(jnp.where(hit, sources[None, :], 0), axis=1)
    where = jnp.sum(jnp.where(hit, mine[None, :], 0), axis=1)
    return order.astype(jnp.int32), source.astype(jnp.int32), where.astype(jnp.int32), piece_starts


def on_device(
    tokens,
    out_grad,
    piece_starts,
    span_order,
    ln1_gain,
    ln1_bias,
    qkv_weight,
    query_bias,
    value_bias,
    out_weight,
    out_bias,
    ln2_gain,
    ln2_bias,
    fc_weight,
    fc_bias,
    proj_weight,
    proj_bias,
):
    core = lax.axis_index("core")
    z_place = lax.axis_index("z")
    x_place = lax.axis_index("x")
    y_place = lax.axis_index(Y)
    sequence = lax.axis_index("yl")
    head_part = x_place // 2
    query_part = x_place % 2
    places = jnp.stack([y_place, x_place, z_place, core]).astype(jnp.int32)
    own = tokens[0]
    dm_own = out_grad[0]

    both_tables = lax.all_gather(
        jnp.concatenate([span_order[0], piece_starts[0]]), "core", axis=0, tiled=False
    )
    table = lax.dynamic_index_in_dim(both_tables, sequence, 0, keepdims=False)
    tables = order_tables(table[:64], table[64:], query_part)

    qkv_parts = qkv_weight[0].reshape(8, 3, 2, 2, 2, 2, 64)
    kv_cols = qkv_parts[:, 1:].transpose(3, 2, 4, 0, 5, 1, 6).reshape(2, 4, 8, 256)
    q_cols = qkv_parts[:, 0].transpose(2, 1, 3, 0, 4, 5).reshape(2, 4, 8, 128)
    fc_cols = fc_weight[0].reshape(8, 2, 2, 2, 512).transpose(2, 1, 3, 0, 4).reshape(2, 4, 8, 512)
    out_cols = jnp.broadcast_to(
        out_weight[0].reshape(8, 4, 256).transpose(1, 0, 2)[None], (2, 4, 8, 256)
    )
    vectors = jnp.stack(
        [
            ln1_gain[0],
            ln1_bias[0],
            query_bias[0],
            value_bias[0],
            out_bias[0],
            ln2_gain[0],
            ln2_bias[0],
            proj_bias[0],
        ],
        axis=1,
    )
    vectors = jnp.concatenate(
        [vectors, fc_bias[0].reshape(8, 4), jnp.zeros((8, 116), BF)], axis=1
    )
    vec_cols = jnp.broadcast_to(vectors[None, None], (2, 4, 8, 128))
    packed = jnp.concatenate([kv_cols, q_cols, vec_cols, fc_cols, out_cols], axis=3)
    spread = lax.all_to_all(
        packed.reshape(8, 8, 1280), ("core", "z"), split_axis=0, concat_axis=0, tiled=True
    )

    first = ring_stack(spread[:, :, :512].reshape(64, 512), "x")
    first = place_call(place_first, places, ring_blocks(first, Y), [(1024, 512)])[0]
    qkv_matrix = first[:, :384]
    rows = first[:, 384:396].T
    first_gain, first_shift, q_shift, v_shift, out_shift, gain_two, shift_two, proj_shift = [
        rows[i].astype(F32) for i in range(8)
    ]
    fc_shift = first[:, 392:396].reshape(4096)

    out_mine = lax.dynamic_index_in_dim(
        spread[:, :, 1024:].reshape(2, 32, 256), core, 0, keepdims=False
    )
    out_mine = out_mine.reshape(2, 16, 256).transpose(1, 0, 2).reshape(16, 512)
    second = jnp.concatenate([spread[:, :, 512:1024].reshape(64, 512), out_mine], axis=0)
    second = ring_stack(second, "x")
    second = ring_stack(second, Y)
    fc_matrix, out_matrix = place_call(
        place_second, places, ring_blocks(second, "z"), [(4, 1024, 512), (512, 1024)]
    )
    third = ring_stack(proj_weight[0], "z")
    third = ring_stack(third, "x")
    proj_matrix = place_call(place_third, places, ring_blocks(third, Y), [(4, 512, 1024)])[0]

    rows_z = ring_stack(own, "z")
    group = place_call(place_rows, places, [rows_z, swap_core(rows_z)], [(2, 4, 128, 1024)])[0]
    group = group.reshape(1024, D)
    normed = layer_norm(group.astype(F32), first_gain, first_shift).astype(BF)
    projected = plain_product(normed, qkv_matrix)

    def head_columns(vector):
        parts = vector.reshape(2, 2, 2, 128)
        parts = parts.transpose(1, 0, 2, 3).reshape(8, 128)
        return lax.dynamic_index_in_dim(parts, core * 4 + z_place, 0, keepdims=False)

    q_add = head_columns(q_shift)
    v_add = head_columns(v_shift)
    zero = jnp.zeros((64,), F32)
    add = jnp.concatenate([zero, v_add[:64], zero, v_add[64:], q_add])
    projected = (projected + add).astype(BF)
    kv_msg = projected[:, :256].reshape(2, 512, 2, 128).transpose(0, 2, 1, 3)
    kv_msg = jnp.broadcast_to(kv_msg[:, :, None], (2, 2, 2, 512, 128))
    q_msg = (
        projected[:, 256:]
        .reshape(2, 4, 2, 2, 32, 2, 64)
        .transpose(0, 5, 2, 1, 4, 3, 6)
        .reshape(2, 2, 2, 128, 128)
    )
    msg = jnp.concatenate([kv_msg, q_msg], axis=3).reshape(8, 640, 128)
    got = lax.all_to_all(msg, ("yl", "x"), split_axis=0, concat_axis=0, tiled=True)

    kv, query, mix, log_total, o_msg = attend_forward(tables, got)
    o_got = lax.all_to_all(o_msg, ("yl", "x", "z"), split_axis=0, concat_axis=0, tiled=True)
    o_rows = (
        o_got.reshape(2, 2, 2, 4, 32, 2, 64).transpose(0, 2, 5, 4, 3, 1, 6).reshape(2, 128, 512)
    )
    o_two = jnp.concatenate(
        [jnp.where(core == 0, o_rows[0], o_rows[1]), jnp.where(core == 0, o_rows[1], o_rows[0])]
    )

    dm_two = jnp.concatenate([dm_own, swap_core(dm_own)], axis=0)
    part = plain_product(o_two, out_matrix)
    middle = own.astype(F32) + (part[:128] + swap_core(part[128:]) + out_shift)
    a2_own = layer_norm(middle, gain_two, shift_two).astype(BF)
    a2_two = jnp.concatenate([a2_own, swap_core(a2_own)], axis=0)

    fc_local = lax.dynamic_index_in_dim(
        fc_shift.reshape(2, 2, 1024), core, 1, keepdims=False
    ).reshape(4, 512)
    next_part = jnp.zeros((256, D), F32)
    da2_part = jnp.zeros((256, D), F32)
    dfc_list, dproj_list, dfc_shift_list = [], [], []
    for block in range(4):
        pre = plain_product(a2_two, fc_matrix[block]) + fc_local[block].astype(F32)
        act, back = jax.vjp(gelu_tanh, pre)
        act = act.astype(BF)
        next_part += plain_product(act, proj_matrix[block])
        dact = right_product(dm_two, proj_matrix[block])
        df = back(dact)[0].astype(BF)
        da2_part += right_product(df, fc_matrix[block])
        dproj_list.append(left_product(act, dm_two).astype(BF))
        dfc_list.append(left_product(a2_two, df).astype(BF))
        dfc_shift_list.append(jnp.sum(df.astype(F32), axis=0))
    final = middle + (next_part[:128] + swap_core(next_part[128:]) + proj_shift)
    da2 = da2_part[:128] + swap_core(da2_part[128:])
    back_two, normed_two = norm_backward(middle, gain_two, da2)
    dmid = dm_own.astype(F32) + back_two
    da_own = dmid.astype(BF)
    da_two = jnp.concatenate([da_own, swap_core(da_own)], axis=0)
    dout = left_product(o_two, da_two).astype(BF)
    do_two = right_product(da_two, out_matrix).astype(BF).reshape(2, 128, 512)
    do_rows = jnp.stack(
        [jnp.where(core == 0, do_two[0], do_two[1]), jnp.where(core == 0, do_two[1], do_two[0])]
    )
    do_msg = (
        do_rows.reshape(2, 2, 2, 32, 4, 2, 64).transpose(0, 5, 1, 4, 3, 2, 6).reshape(32, 32, 128)
    )
    do_got = lax.all_to_all(do_msg, ("yl", "x", "z"), split_axis=0, concat_axis=0, tiled=True)

    dproj = jnp.stack(dproj_list).reshape(4, 4, 4, 32, 1024)
    dproj = ring_reduce(dproj, Y)
    dproj = ring_reduce(dproj, "x")
    dproj = ring_reduce(dproj, "z")
    dfc = jnp.stack(dfc_list).reshape(4, 2, 2, 8, 32, 512).transpose(0, 1, 3, 2, 4, 5)
    dout_parts = (
        dout.reshape(4, 4, 2, 16, 4, 256).transpose(4, 0, 1, 3, 2, 5).reshape(4, 4, 4, 16, 512)
    )
    dsecond = jnp.concatenate([dfc.reshape(4, 4, 4, 64, 512), dout_parts], axis=3)
    dsecond = ring_reduce(dsecond, "z")
    dsecond = ring_reduce(dsecond, Y)
    dsecond = ring_reduce(dsecond, "x")

    dmsg = attend_backward(tables, (kv, query, mix, log_total), do_got)
    dgot = lax.all_to_all(dmsg, ("yl", "x"), split_axis=0, concat_axis=0, tiled=True)
    dgot = dgot.reshape(2, 2, 2, 640, 128)
    dkv = (dgot[:, :, 0, :512].astype(F32) + dgot[:, :, 1, :512].astype(F32)).astype(BF)
    dkv = dkv.transpose(0, 2, 1, 3).reshape(1024, 256)
    dq = (
        dgot[:, :, :, 512:]
        .reshape(2, 2, 2, 4, 32, 2, 64)
        .transpose(0, 3, 2, 5, 4, 1, 6)
        .reshape(1024, 128)
    )
    dqkv = jnp.concatenate([dkv, dq], axis=1)
    dqkv_matrix = left_product(normed, dqkv).astype(BF)
    da1_part = right_product(dqkv, qkv_matrix)
    group32 = group.astype(F32)
    center = group32 - jnp.mean(group32, axis=-1, keepdims=True)
    normed_one = center * lax.rsqrt(jnp.mean(center * center, axis=-1, keepdims=True) + EPS)
    dgain_one = jnp.sum(da1_part * normed_one, axis=0)
    dshift_one = jnp.sum(da1_part, axis=0)
    halves = da1_part.astype(BF).reshape(2, 4, 128, D)
    mine = lax.dynamic_index_in_dim(halves, core, 0, keepdims=False)
    other = swap_core(lax.dynamic_index_in_dim(halves, 1 - core, 0, keepdims=False))
    da1 = ring_reduce((mine.astype(F32) + other.astype(F32)).astype(BF), "z").astype(F32)
    back_one, _ = norm_backward(own.astype(F32), first_gain, da1)
    dtokens = dmid + back_one

    def spread_columns(sums):
        chunk = lax.broadcasted_iota(jnp.int32, (8, 1), 0)
        parts = jnp.where(chunk == core * 4 + z_place, sums[None, :], 0.0)
        return parts.reshape(2, 2, 2, 128).transpose(1, 0, 2, 3).reshape(1024)

    qkv_sums = jnp.sum(dqkv.astype(F32), axis=0)
    dq_shift = spread_columns(qkv_sums[256:])
    dv_shift = spread_columns(jnp.concatenate([qkv_sums[64:128], qkv_sums[192:256]]))
    dfc_shift = jnp.stack(dfc_shift_list).reshape(2, 1, 1024)
    side = lax.broadcasted_iota(jnp.int32, (1, 2, 1), 1)
    dfc_shift = jnp.where(side == core, dfc_shift, 0.0).reshape(1024, 4)
    columns = jnp.stack(
        [
            dgain_one,
            dshift_one,
            dq_shift,
            dv_shift,
            jnp.sum(da_own.astype(F32), axis=0),
            jnp.sum(da2 * normed_two, axis=0),
            jnp.sum(da2, axis=0),
            jnp.sum(dm_own.astype(F32), axis=0),
        ],
        axis=1,
    )
    columns = jnp.concatenate([columns, dfc_shift, jnp.zeros((1024, 116), F32)], axis=1)
    dfirst = jnp.concatenate([dqkv_matrix, columns.astype(BF)], axis=1)
    dfirst = dfirst.reshape(2, 2, 8, 32, 512).transpose(0, 2, 1, 3, 4).reshape(4, 4, 64, 512)
    dfirst = ring_reduce(dfirst, Y)
    dfirst = ring_reduce(dfirst, "x")

    dout_mine = dsecond[64:].reshape(16, 2, 256).transpose(1, 0, 2).reshape(1, 32, 256)
    dout_both = jnp.broadcast_to(dout_mine, (2, 32, 256)).reshape(8, 8, 256)
    back = jnp.concatenate(
        [dfirst.reshape(8, 8, 512), dsecond[:64].reshape(8, 8, 512), dout_both], axis=2
    )
    back = lax.all_to_all(back, ("core", "z"), split_axis=0, concat_axis=0, tiled=True).astype(F32)
    kv_back = back[:, :, :256].reshape(2, 2, 2, 8, 2, 2, 64).transpose(3, 5, 1, 0, 2, 4, 6)
    q_back = back[:, :, 256:384].reshape(2, 2, 2, 8, 2, 64).transpose(3, 1, 0, 2, 4, 5)
    grad_qkv = jnp.concatenate([q_back.reshape(8, 1024), kv_back.reshape(8, 2048)], axis=1)
    grad_fc = back[:, :, 512:1024].reshape(2, 2, 2, 8, 512).transpose(3, 1, 0, 2, 4).reshape(8, 4096)
    out_back = lax.dynamic_index_in_dim(
        back[:, :, 1024:].reshape(2, 4, 8, 256), core, 0, keepdims=False
    )
    grad_out = out_back.transpose(1, 0, 2).reshape(8, 1024)
    sums = jnp.sum(back[:, :, 384:396], axis=0)
    vecs = [sums[:, i][None] for i in range(8)]
    return (
        final.astype(BF)[None],
        dtokens[None],
        vecs[0],
        vecs[1],
        grad_qkv[None],
        vecs[2],
        vecs[3],
        grad_out[None],
        vecs[4],
        vecs[5],
        vecs[6],
        grad_fc[None],
        sums[:, 8:].reshape(1, 32),
        dproj.astype(F32)[None],
        vecs[7],
    )


def solution(mesh):
    fine = Mesh(mesh.devices.reshape(2, 2, 2, 4, 4), AXES)
    dp, seq, every = ("yh", "core"), ("yl", "x", "z"), AXES
    vector, matrix, tokens = P(None, every), P(None, every, None), P(dp, seq, None)
    return jax.shard_map(
        on_device,
        mesh=fine,
        in_specs=(
            tokens,
            tokens,
            P(dp, None),
            P(dp, None),
            vector,
            vector,
            matrix,
            vector,
            vector,
            matrix,
            vector,
            vector,
            vector,
            matrix,
            vector,
            matrix,
            vector,
        ),
        out_specs=(
            tokens,
            tokens,
            vector,
            vector,
            matrix,
            vector,
            vector,
            matrix,
            vector,
            vector,
            vector,
            matrix,
            vector,
            matrix,
            vector,
        ),
        check_vma=False,
    )
```

```python
import functools

import jax
import jax.numpy as jnp
from jax import lax
from jax.experimental import pallas as pl
from jax.experimental.pallas import tpu as pltpu
from jax.sharding import Mesh, PartitionSpec as P

D = 1024
PIECE = 256
EPS = 1e-05
NEG = -1e30
LOG2E = 1.4426950408889634
BF = jnp.bfloat16
F32 = jnp.float32
AXES = ("yh", "core", "yl", "x", "z")
PLANE = ("yh", "yl", "x")
Y = ("yh", "yl")
QB = 256
KB = 512


def plain_product(left_side, right_side):
    return jnp.dot(left_side, right_side, preferred_element_type=F32)


def left_product(left_side, right_side):
    return lax.dot_general(
        left_side, right_side, (((0,), (0,)), ((), ())), preferred_element_type=F32
    )


def right_product(left_side, right_side):
    return lax.dot_general(
        left_side, right_side, (((1,), (1,)), ((), ())), preferred_element_type=F32
    )


def layer_norm(values, gain, shift):
    center = values - jnp.mean(values, axis=-1, keepdims=True)
    spread = jnp.mean(center * center, axis=-1, keepdims=True)
    return center * lax.rsqrt(spread + EPS) * gain + shift


def norm_backward(values, gain, grad):
    center = values - jnp.mean(values, axis=-1, keepdims=True)
    spread = jnp.mean(center * center, axis=-1, keepdims=True)
    scale = lax.rsqrt(spread + EPS)
    normed = center * scale
    pulled = grad * gain
    back = scale * (
        pulled
        - jnp.mean(pulled, axis=-1, keepdims=True)
        - normed * jnp.mean(pulled * normed, axis=-1, keepdims=True)
    )
    return back, normed


def shift(values, axis, step):
    return lax.ppermute(values, axis, [(i, (i + step) % 4) for i in range(4)])


def swap_core(values):
    return lax.ppermute(values, "core", [(0, 1), (1, 0)])


def ring_blocks(values, axis):
    return [values, shift(values, axis, -1), shift(values, axis, 2), shift(values, axis, 1)]


def ring_stack(values, axis):
    return jnp.stack(ring_blocks(values, axis))


def add_all(terms):
    total = terms[0].astype(F32)
    for term in terms[1:]:
        total = total + term.astype(F32)
    return total.astype(BF)


def ring_reduce(blocks, axis):
    return add_all(ring_arrive(blocks, axis))


def ring_arrive(blocks, axis):
    return [
        blocks[0],
        shift(blocks[1], axis, 1),
        shift(blocks[2], axis, 2),
        shift(blocks[3], axis, -1),
    ]


def exchange(values, axes):
    return lax.all_to_all(values, axes, split_axis=0, concat_axis=0, tiled=True)


def spread_out(values, axes, count):
    return exchange(jnp.broadcast_to(values[None], (count,) + values.shape), axes)


def around(place, step):
    return lax.rem(place + step, 4)


def feature_row(y, side, x):
    return (y // 2) * 512 + side * 256 + (y % 2) * 128 + x * 32


def cost(microseconds):
    return pl.CostEstimate(
        flops=microseconds * 1_000_000_000, bytes_accessed=1, transcendentals=0
    )


def vmem_call(kernel, out_shape, places, arrays, scratch=(), after=(), microseconds=2):
    count = len(arrays)

    def body(*refs):
        kernel(*refs[: 1 + count], *refs[1 + count + len(after) :])

    return pl.pallas_call(
        body,
        out_shape=[jax.ShapeDtypeStruct(shape, dtype) for shape, dtype in out_shape],
        in_specs=[pl.BlockSpec(memory_space=pltpu.SMEM)]
        + [pl.BlockSpec(memory_space=pltpu.VMEM)] * count
        + [pl.BlockSpec(memory_space=pl.ANY)] * len(after),
        out_specs=[pl.BlockSpec(memory_space=pltpu.VMEM)] * len(out_shape),
        scratch_shapes=[pltpu.VMEM(shape, dtype) for shape, dtype in scratch],
        cost_estimate=cost(microseconds),
        compiler_params=pltpu.CompilerParams(vmem_limit_bytes=50 * 1024 * 1024),
    )(places, *arrays, *after)


def tie_kernel(*refs):
    pass


def tie(values, *after):
    return pl.pallas_call(
        tie_kernel,
        out_shape=jax.ShapeDtypeStruct(values.shape, values.dtype),
        in_specs=[pl.BlockSpec(memory_space=pl.ANY)] * (1 + len(after)),
        out_specs=pl.BlockSpec(memory_space=pl.ANY),
        input_output_aliases={0: 0},
    )(values, *after)


def lane_half(shape):
    return lax.broadcasted_iota(jnp.int32, shape, 1) < 64


def head_lanes(places):
    z, core = places[2], places[3]
    return pl.multiple_of((z // 2) * 512 + core * 256 + (z % 2) * 128, 128)


def qkv_kernel(places, source_weight, own, other, msg, normed, weight, rows):
    for chip in range(16):
        for side in range(2):
            row = feature_row(chip // 4, side, chip % 4)
            weight[row : row + 32, :] = source_weight[chip, side * 32 : side * 32 + 32, :]
    vectors = weight[:, 384:512].astype(F32)
    rows[...] = jnp.transpose(vectors)[0:16, :]
    gain, shift_row = rows[0:1, :], rows[1:2, :]
    lanes = pl.ds(head_lanes(places), 128)
    query_add = rows[2:3, lanes]
    value_add = jnp.broadcast_to(rows[3:4, lanes], (8, 128))
    left8 = lane_half((8, 128))
    first_add = jnp.where(left8, 0.0, pltpu.roll(value_add, 64, 1))[0:1]
    second_add = jnp.where(left8, 0.0, value_add)[0:1]
    left = lane_half((32, 128))
    for side, source in enumerate((own, other)):
        sequence = places[3] if side == 0 else 1 - places[3]
        for step in range(4):
            z = around(places[2], step)
            values = source[step].astype(F32)
            center = values - jnp.mean(values, axis=1, keepdims=True)
            spread = jnp.mean(center * center, axis=1, keepdims=True)
            row = (center * lax.rsqrt(spread + EPS) * gain + shift_row).astype(BF)
            normed[sequence, z] = row
            made = plain_product(row, weight[:, 0:384])
            pairs = (
                (made[:, 0:128] + first_add).astype(BF),
                (made[:, 128:256] + second_add).astype(BF),
            )
            query = made[:, 256:384] + query_add
            turned = pltpu.roll(query, 64, 1)
            begin = pl.multiple_of(z * 128, 128)
            q_begin = pl.multiple_of(512 + z * 32, 32)
            for part in range(2):
                top, bottom = part * 64, part * 64 + 32
                packed = (
                    jnp.where(left, query[top : top + 32], turned[bottom : bottom + 32]),
                    jnp.where(left, turned[top : top + 32], query[bottom : bottom + 32]),
                )
                for head in range(2):
                    task = sequence * 4 + head * 2 + part
                    msg[task, pl.ds(begin, 128), :] = pairs[head]
                    msg[task, pl.ds(q_begin, 32), :] = packed[head].astype(BF)


def out_kernel(places, got, b0, b1, b2, b3, own, other, attended, matrix):
    for turn, ref in enumerate((b0, b1, b2, b3)):
        x = around(places[1], turn)
        for up in range(4):
            y = around(places[0], up)
            matrix[pl.ds(pl.multiple_of((y * 4 + x) * 32, 32), 32), :] = ref[up]
    left = lane_half((32, 128))
    for side in range(2):
        sequence = places[3] if side == 0 else 1 - places[3]
        for part in range(2):
            for pair in range(4):
                one = got[(sequence * 4 + part) * 4 + pair].astype(F32)
                two = got[(sequence * 4 + 2 + part) * 4 + pair].astype(F32)
                row = side * 128 + part * 64
                columns = slice(pair * 128, pair * 128 + 128)
                attended[row : row + 32, columns] = jnp.where(
                    left, one, pltpu.roll(two, 64, 1)
                ).astype(BF)
                attended[row + 32 : row + 64, columns] = jnp.where(
                    left, pltpu.roll(one, 64, 1), two
                ).astype(BF)
    product = plain_product(attended[...], matrix[...])
    own[...] = product[0:128]
    other[...] = product[128:256]


def feed_kernel(
    places,
    a2_own,
    a2_other,
    dm_own,
    dm_other,
    bias,
    w0,
    w1,
    w2,
    w3,
    next_own,
    next_other,
    da2_own,
    da2_other,
    sums,
    bias_sum,
    fc,
    proj,
    act_all,
    df_all,
):
    for up, weights in enumerate((w0, w1, w2, w3)):
        y = around(places[0], up)
        for turn in range(4):
            x = around(places[1], turn)
            for side in range(2):
                fc[pl.ds(pl.multiple_of(feature_row(y, side, x), 32), 32), :] = weights[
                    turn, side * 32 : side * 32 + 32, :
                ]
                proj[
                    pl.ds(pl.multiple_of((y * 4 + x) * 32, 32), 32),
                    side * 512 : side * 512 + 512,
                ] = weights[turn, 64 + side * 32 : 96 + side * 32, :]
    total = jnp.zeros((1, 512), F32)
    for half in range(4):
        a2, dm = (a2_own, dm_own) if half < 2 else (a2_other, dm_other)
        part = slice(half % 2 * 2, half % 2 * 2 + 2)
        a2_rows = a2[part].reshape(256, D)
        dm_rows = dm[part].reshape(256, D)
        pre = plain_product(a2_rows, fc[...]) + bias[0:1, :]
        square = pre * pre
        bent = jnp.tanh(0.7978845608028654 * pre * (1.0 + 0.044715 * square))
        side = 0.5 * (1.0 + bent)
        act = (pre * side).astype(BF)
        slope = side + 0.5 * pre * (1.0 - bent * bent) * (
            0.7978845608028654 * (1.0 + 0.134145 * square)
        )
        df = (right_product(dm_rows, proj[...]) * slope).astype(BF)
        rows = slice(half * 256, half * 256 + 256)
        act_all[rows] = act
        df_all[rows] = df
        total += jnp.sum(df.astype(F32), axis=0, keepdims=True)
        made = plain_product(act, proj[...]).reshape(2, 128, D)
        pulled = right_product(df, fc[...]).reshape(2, 128, D)
        if half < 2:
            next_own[part] = made
            da2_own[part] = pulled
        else:
            next_other[part] = made.astype(BF)
            da2_other[part] = pulled.astype(BF)
    bias_sum[...] = jnp.broadcast_to(total, (8, 512))
    fc_sum = left_product(a2_own[...].reshape(512, D), df_all[0:512]) + left_product(
        a2_other[...].reshape(512, D), df_all[512:1024]
    )
    proj_sum = left_product(act_all[0:512], dm_own[...].reshape(512, D)) + left_product(
        act_all[512:1024], dm_other[...].reshape(512, D)
    )
    for chip in range(16):
        for side in range(2):
            row = feature_row(chip // 4, side, chip % 4)
            sums[chip, side * 32 : side * 32 + 32, :] = fc_sum[row : row + 32].astype(BF)
            sums[chip, 64 + side * 32 : 96 + side * 32, :] = proj_sum[
                chip * 32 : chip * 32 + 32, side * 512 : side * 512 + 512
            ].astype(BF)


def attended_grad_kernel(places, da, matrix, msg):
    product = right_product(da[...], matrix[...])
    turned = [pltpu.roll(product[:, i * 128 : i * 128 + 128], 64, 1) for i in range(4)]
    left = lane_half((32, 128))
    for side in range(2):
        sequence = places[3] if side == 0 else 1 - places[3]
        for part in range(2):
            for pair in range(4):
                top = side * 128 + part * 64
                bottom = top + 32
                flat = product[:, pair * 128 : pair * 128 + 128]
                msg[(sequence * 4 + part) * 4 + pair] = jnp.where(
                    left, flat[top : top + 32], turned[pair][bottom : bottom + 32]
                ).astype(BF)
                msg[(sequence * 4 + 2 + part) * 4 + pair] = jnp.where(
                    left, turned[pair][top : top + 32], flat[bottom : bottom + 32]
                ).astype(BF)


def out_grad_kernel(places, attended, da, o0, o1, o2, o3, total):
    total[...] = left_product(attended[...], da[...])
    for step, ref in enumerate((o0, o1, o2, o3)):
        z = around(places[2], step)
        ref[...] = jnp.concatenate(
            [total[pl.ds(pl.multiple_of(chip * 32 + z * 8, 8), 8), :] for chip in range(16)], axis=0
        ).astype(BF)


def input_grad_kernel(
    places, got, own, other, normed, weight, sums, dout, da_own, da_other, weight_sum, rows, dqkv, total
):
    left = lane_half((32, 128))
    for sequence in range(2):
        for head in range(2):
            task = (sequence * 2 + head) * 2
            dqkv[sequence * 512 : sequence * 512 + 512, head * 128 : head * 128 + 128] = (
                got[task, 0:512, :].astype(F32) + got[task + 1, 0:512, :].astype(F32)
            ).astype(BF)
        for part in range(2):
            for z in range(4):
                at = slice(512 + z * 32, 544 + z * 32)
                one = got[sequence * 4 + part, at, :].astype(F32)
                two = got[sequence * 4 + 2 + part, at, :].astype(F32)
                row = sequence * 512 + z * 128 + part * 64
                dqkv[row : row + 32, 256:384] = jnp.where(
                    left, one, pltpu.roll(two, 64, 1)
                ).astype(BF)
                dqkv[row + 32 : row + 64, 256:384] = jnp.where(
                    left, pltpu.roll(one, 64, 1), two
                ).astype(BF)
    column = jnp.sum(dqkv[...].astype(F32), axis=0, keepdims=True)
    column = jnp.broadcast_to(column, (8, 384))
    left8 = lane_half((8, 128))
    value_sum = jnp.where(left8, pltpu.roll(column[:, 0:128], 64, 1), column[:, 128:256])
    gain_sum = jnp.zeros((1, D), F32)
    shift_sum = jnp.zeros((1, D), F32)
    for side, source in enumerate((own, other)):
        sequence = places[3] if side == 0 else 1 - places[3]
        for step in range(4):
            z = around(places[2], step)
            begin = pl.multiple_of(sequence * 512 + z * 128, 128)
            grad = right_product(dqkv[pl.ds(begin, 128), :], weight[:, 0:384])
            values = source[step].astype(F32)
            center = values - jnp.mean(values, axis=1, keepdims=True)
            spread = jnp.mean(center * center, axis=1, keepdims=True)
            gain_sum += jnp.sum(grad * (center * lax.rsqrt(spread + EPS)), axis=0, keepdims=True)
            shift_sum += jnp.sum(grad, axis=0, keepdims=True)
            if side == 0:
                da_own[step] = grad
            else:
                da_other[step] = grad.astype(BF)
    rows[...] = sums[...]
    rows[0:1, :] = gain_sum
    rows[1:2, :] = shift_sum
    lanes = pl.ds(head_lanes(places), 128)
    rows[2:4, :] = jnp.zeros((2, D), F32)
    rows[2:3, lanes] = column[0:1, 256:384]
    rows[3:4, lanes] = value_sum[0:1]
    total[:, 0:384] = left_product(normed[...].reshape(1024, D), dqkv[...]).astype(BF)
    total[:, 384:512] = jnp.transpose(
        jnp.concatenate([rows[...], jnp.zeros((112, D), F32)], axis=0)
    ).astype(BF)
    for chip in range(16):
        for side in range(2):
            row = feature_row(chip // 4, side, chip % 4)
            weight_sum[chip, side * 32 : side * 32 + 32, :] = total[row : row + 32, :]
        weight_sum[chip, 64:80, :] = dout[chip]


def limit_of(position, starts):
    limit = position
    for start in starts:
        limit = jnp.where((position >= start) & (position < start + PIECE), start + PIECE - 1, limit)
    return limit


def forward_kernel(order_ref, source_ref, where_ref, starts_ref, got_ref, *refs):
    kv_ref, q_ref, o_ref, lse_ref, msg_ref = refs[-5:]
    starts = [starts_ref[i] for i in range(6)]

    @pl.loop(0, 64)
    def _(span):
        stored = order_ref[span]
        kv_ref[pl.ds(pl.multiple_of(span * 64, 64), 64), :] = got_ref[
            stored // 8, pl.ds(pl.multiple_of((stored % 8) * 64, 64), 64), :
        ]

    @pl.loop(0, 32)
    def _(span):
        source = source_ref[span]
        packed = got_ref[
            source // 4, pl.ds(pl.multiple_of(512 + (source % 4) * 32, 32), 32), :
        ].astype(F32) * 0.125
        left = lane_half(packed.shape)
        row = pl.multiple_of(span * 64, 64)
        q_ref[pl.ds(row, 32), :] = jnp.where(left, packed, 0.0).astype(BF)
        q_ref[pl.ds(row + 32, 32), :] = jnp.where(left, pltpu.roll(packed, 64, 1), 0.0).astype(BF)

    @pl.loop(0, 2048 // QB)
    def _(block):
        row = pl.multiple_of(block * QB, QB)
        query = q_ref[pl.ds(row, QB), :]
        spans = QB // 64
        first = limit_of(where_ref[block * spans] * 64, starts)
        last = limit_of(where_ref[block * spans + spans - 1] * 64 + 63, starts)
        full = (first + 1) // KB
        count = last // KB + 1
        inner = lax.broadcasted_iota(jnp.int32, (64, 1), 0)
        position = jnp.concatenate(
            [where_ref[block * spans + i] * 64 + inner for i in range(spans)], axis=0
        )
        limit = limit_of(position, starts)

        def step(masked, index, carry):
            maxima, totals, mixture = carry
            begin = pl.multiple_of(index * KB, KB)
            pair = kv_ref[pl.ds(begin, KB), :]
            scores = right_product(query, pair)
            if masked:
                key_pos = begin + lax.broadcasted_iota(jnp.int32, (1, KB), 1)
                scores = jnp.where(key_pos <= limit, scores, NEG)
            higher = jnp.maximum(maxima, jnp.max(scores, axis=1, keepdims=True))
            raised = jnp.exp2((scores - higher) * LOG2E)
            fade = jnp.exp2((maxima - higher) * LOG2E)
            totals = totals * fade + jnp.sum(raised, axis=1, keepdims=True)
            mixture = mixture * fade + plain_product(raised.astype(BF), pair)
            return higher, totals, mixture

        carry = (
            jnp.full((QB, 1), NEG, F32),
            jnp.zeros((QB, 1), F32),
            jnp.zeros((QB, 128), F32),
        )
        carry = lax.fori_loop(0, full, functools.partial(step, False), carry)
        maxima, totals, mixture = lax.fori_loop(full, count, functools.partial(step, True), carry)
        attended = mixture / totals
        o_ref[pl.ds(row, QB), :] = attended.astype(BF)
        log_total = maxima * LOG2E + jnp.log2(totals)
        lse_ref[block] = jnp.transpose(jnp.broadcast_to(log_total, (QB, 128)))[0:8, :]
        turned = pltpu.roll(attended, 64, 1)
        for i in range(spans):
            top, bottom = turned[i * 64 : i * 64 + 32], attended[i * 64 + 32 : i * 64 + 64]
            msg_ref[source_ref[block * spans + i]] = jnp.where(
                lane_half(top.shape), top, bottom
            ).astype(BF)


def backward_kernel(
    order_ref,
    source_ref,
    where_ref,
    starts_ref,
    kv_ref,
    q_ref,
    o_ref,
    lse_ref,
    got_ref,
    *refs,
):
    msg_ref, do_ref, sum_ref = refs[-3:]
    starts = [starts_ref[i] for i in range(6)]

    @pl.loop(0, 32)
    def _(span):
        packed = got_ref[source_ref[span]].astype(F32)
        left = lane_half(packed.shape)
        row = pl.multiple_of(span * 64, 64)
        do_ref[pl.ds(row, 32), :] = jnp.where(left, 0.0, pltpu.roll(packed, 64, 1)).astype(BF)
        do_ref[pl.ds(row + 32, 32), :] = jnp.where(left, 0.0, packed).astype(BF)

    sum_ref[...] = jnp.zeros_like(sum_ref)

    @pl.loop(0, 2048 // QB)
    def _(block):
        row = pl.multiple_of(block * QB, QB)
        query = q_ref[pl.ds(row, QB), :]
        grad = do_ref[pl.ds(row, QB), :]
        both = jnp.concatenate([query, grad], axis=0)
        spans = QB // 64
        first = limit_of(where_ref[block * spans] * 64, starts)
        last = limit_of(where_ref[block * spans + spans - 1] * 64 + 63, starts)
        full = (first + 1) // KB
        count = last // KB + 1
        inner = lax.broadcasted_iota(jnp.int32, (1, 64), 1)
        position = jnp.concatenate(
            [where_ref[block * spans + i] * 64 + inner for i in range(spans)], axis=1
        )
        limit = limit_of(position, starts)
        log_total = lse_ref[block][0:1, :]
        product = grad.astype(F32) * o_ref[pl.ds(row, QB), :].astype(F32)
        delta = lax.dot_general(
            jnp.ones((8, 128), F32),
            product,
            (((1,), (1,)), ((), ())),
            precision=lax.Precision.HIGHEST,
            preferred_element_type=F32,
        )[0:1, :]

        def step(masked, index, total):
            begin = pl.multiple_of(index * KB, KB)
            pair = kv_ref[pl.ds(begin, KB), :]
            scores = right_product(pair, query)
            if masked:
                key_pos = begin + lax.broadcasted_iota(jnp.int32, (KB, 1), 0)
                scores = jnp.where(key_pos <= limit, scores, NEG)
            weights = jnp.exp2(scores * LOG2E - log_total)
            grad_scores = (weights * (right_product(pair, grad) - delta)).astype(BF)
            sum_ref[pl.ds(begin, KB), :] += plain_product(
                jnp.concatenate([grad_scores, weights.astype(BF)], axis=1), both
            )
            return total + left_product(grad_scores, pair)

        total = jnp.zeros((QB, 128), F32)
        total = lax.fori_loop(0, full, functools.partial(step, False), total)
        total = lax.fori_loop(full, count, functools.partial(step, True), total) * 0.125
        turned = pltpu.roll(total, 64, 1)
        for i in range(spans):
            top, bottom = total[i * 64 : i * 64 + 32], turned[i * 64 + 32 : i * 64 + 64]
            source = source_ref[block * spans + i]
            msg_ref[
                source // 4, pl.ds(pl.multiple_of(512 + (source % 4) * 32, 32), 32), :
            ] = jnp.where(lane_half(top.shape), top, bottom).astype(BF)

    @pl.loop(0, 64)
    def _(span):
        stored = order_ref[span]
        msg_ref[stored // 8, pl.ds(pl.multiple_of((stored % 8) * 64, 64), 64), :] = sum_ref[
            pl.ds(pl.multiple_of(span * 64, 64), 64), :
        ].astype(BF)


def attend_forward(tables, got, after):
    shapes = [
        jax.ShapeDtypeStruct((4096, 128), BF),
        jax.ShapeDtypeStruct((2048, 128), BF),
        jax.ShapeDtypeStruct((2048, 128), BF),
        jax.ShapeDtypeStruct((2048 // QB, 8, QB), F32),
        jax.ShapeDtypeStruct((32, 32, 128), BF),
    ]
    return pl.pallas_call(
        forward_kernel,
        out_shape=shapes,
        in_specs=[pl.BlockSpec(memory_space=pltpu.SMEM)] * 4
        + [pl.BlockSpec(memory_space=pltpu.VMEM)]
        + [pl.BlockSpec(memory_space=pl.ANY)] * len(after),
        out_specs=[pl.BlockSpec(memory_space=pltpu.VMEM)] * 5,
        cost_estimate=cost(25),
        compiler_params=pltpu.CompilerParams(vmem_limit_bytes=48 * 1024 * 1024),
    )(*tables, got, *after)


def attend_backward(tables, saved, got, after):
    return pl.pallas_call(
        backward_kernel,
        out_shape=jax.ShapeDtypeStruct((8, 640, 128), BF),
        in_specs=[pl.BlockSpec(memory_space=pltpu.SMEM)] * 4
        + [pl.BlockSpec(memory_space=pltpu.VMEM)] * 5
        + [pl.BlockSpec(memory_space=pl.ANY)] * len(after),
        out_specs=pl.BlockSpec(memory_space=pltpu.VMEM),
        scratch_shapes=[pltpu.VMEM((2048, 128), BF), pltpu.VMEM((4096, 128), F32)],
        cost_estimate=cost(25),
        compiler_params=pltpu.CompilerParams(vmem_limit_bytes=48 * 1024 * 1024),
    )(*tables, *saved, got, *after)


def order_tables(span_order, piece_starts, part):
    places = jnp.arange(64, dtype=jnp.int32)
    order = jnp.sum(jnp.where(span_order[None, :] == places[:, None], places[None, :], 0), axis=1)
    mine = lax.dynamic_index_in_dim(span_order.reshape(32, 2), part, 1, keepdims=False)
    rank = jnp.sum((mine[None, :] < mine[:, None]).astype(jnp.int32), axis=1)
    sources = jnp.arange(32, dtype=jnp.int32)
    hit = rank[None, :] == sources[:, None]
    source = jnp.sum(jnp.where(hit, sources[None, :], 0), axis=1)
    where = jnp.sum(jnp.where(hit, mine[None, :], 0), axis=1)
    return order.astype(jnp.int32), source.astype(jnp.int32), where.astype(jnp.int32), piece_starts


def on_device(
    tokens,
    out_grad,
    piece_starts,
    span_order,
    ln1_gain,
    ln1_bias,
    qkv_weight,
    query_bias,
    value_bias,
    out_weight,
    out_bias,
    ln2_gain,
    ln2_bias,
    fc_weight,
    fc_bias,
    proj_weight,
    proj_bias,
):
    core = lax.axis_index("core")
    z_place = lax.axis_index("z")
    x_place = lax.axis_index("x")
    y_place = lax.axis_index(Y)
    sequence = lax.axis_index("yl")
    head_part = x_place // 2
    query_part = x_place % 2
    places = jnp.stack([y_place, x_place, z_place, core]).astype(jnp.int32)
    own = tokens[0]
    dm_own = out_grad[0]

    both_tables = lax.all_gather(
        jnp.concatenate([span_order[0], piece_starts[0]]), "core", axis=0, tiled=False
    )
    table = lax.dynamic_index_in_dim(both_tables, sequence, 0, keepdims=False)
    tables = order_tables(table[:64], table[64:], query_part)

    rows_z = ring_stack(own, "z")
    qkv_parts = qkv_weight[0].reshape(8, 3, 2, 2, 2, 2, 64)
    kv_cols = qkv_parts[:, 1:].transpose(3, 2, 4, 0, 5, 1, 6).reshape(2, 4, 8, 256)
    q_cols = qkv_parts[:, 0].transpose(2, 1, 3, 0, 4, 5).reshape(2, 4, 8, 128)
    fc_cols = (
        fc_weight[0]
        .reshape(8, 2, 2, 2, 4, 4, 32)
        .transpose(2, 5, 0, 1, 3, 4, 6)
        .reshape(2, 4, 8, 512)
    )
    members = (
        ln1_gain,
        ln1_bias,
        query_bias,
        value_bias,
        out_bias,
        ln2_gain,
        ln2_bias,
        proj_bias,
    )
    row_index = lax.broadcasted_iota(jnp.int32, (8, 8), 0)
    vectors = jnp.zeros((8, 8), BF)
    for i, member in enumerate(members):
        vectors = jnp.where(row_index == i, member, vectors)
    vectors = jnp.concatenate(
        [
            vectors.T,
            jnp.zeros((8, 24), BF),
            jnp.pad(fc_bias, ((0, 7), (0, 0))),
            jnp.zeros((8, 64), BF),
        ],
        axis=1,
    )
    vec_cols = jnp.broadcast_to(vectors[None, None], (2, 4, 8, 128))
    packed = jnp.concatenate([kv_cols, q_cols, vec_cols, fc_cols], axis=3)
    spread = lax.all_to_all(
        packed.reshape(8, 8, 1024), ("core", "z"), split_axis=0, concat_axis=0, tiled=True
    )

    out_rows = ring_stack(tie(out_weight[0], spread), "z")
    out_rows = jnp.roll(out_rows, z_place, axis=0).reshape(32, D)
    outs = ring_blocks(ring_stack(out_rows, Y), "x")

    first = spread_out(spread[:, :, :512].reshape(64, 512), PLANE, 16)
    proj_halves = proj_weight[0].reshape(32, 2, 512).transpose(1, 0, 2).reshape(64, 512)
    second = jnp.concatenate([spread[:, :, 512:].reshape(64, 512), proj_halves], axis=0)
    second = ring_blocks(ring_stack(second, "x"), Y)
    rows_other = swap_core(rows_z)
    dm_z = ring_stack(tie(dm_own, first), "z")
    dm_other = swap_core(dm_z)

    msg, normed, qkv_matrix, rows = vmem_call(
        qkv_kernel,
        [
            ((8, 640, 128), BF),
            ((2, 4, 128, D), BF),
            ((1024, 512), BF),
            ((16, D), F32),
        ],
        places,
        [first, rows_z, rows_other],
        microseconds=5,
    )
    got = lax.all_to_all(msg, ("yl", "x"), split_axis=0, concat_axis=0, tiled=True)
    kv, query, mix, log_total, o_msg = attend_forward(
        tables, got, [dm_z, outs[1], outs[2], outs[3]]
    )
    o_got = lax.all_to_all(tie(o_msg, *second[1:]), ("yl", "x", "z"), split_axis=0, concat_axis=0, tiled=True)
    out_shift, gain_two, shift_two, proj_shift = [rows[i] for i in range(4, 8)]
    part_own, part_other, o_two, out_matrix = vmem_call(
        out_kernel,
        [((128, D), F32), ((128, D), F32), ((256, 512), BF), ((512, D), BF)],
        places,
        [o_got, *outs],
    )
    middle = own.astype(F32) + (part_own + swap_core(part_other) + out_shift)
    a2_own = layer_norm(middle, gain_two, shift_two).astype(BF)
    a2_z = ring_stack(a2_own, "z")
    fc_shift = qkv_matrix.reshape(2, 2, 2, 4, 4, 8, 512)[:, :, :, :, :, 0, 416:448]
    fc_shift = lax.dynamic_index_in_dim(fc_shift, core, 1, keepdims=False)
    fc_shift = lax.dynamic_index_in_dim(fc_shift, z_place, 3, keepdims=False)
    fc_shift = jnp.broadcast_to(fc_shift.reshape(1, 512).astype(F32), (8, 512))
    next_own, next_other, da2_own, da2_other, dsecond, bias_sum = vmem_call(
        feed_kernel,
        [
            ((4, 128, D), F32),
            ((4, 128, D), BF),
            ((4, 128, D), F32),
            ((4, 128, D), BF),
            ((16, 128, 512), BF),
            ((8, 512), F32),
        ],
        places,
        [a2_z, swap_core(a2_z), dm_z, dm_other, fc_shift, *second],
        [((1024, 512), BF), ((512, D), BF), ((1024, 512), BF), ((1024, 512), BF)],
        microseconds=12,
    )
    da2_got = swap_core(da2_other)
    da2 = ring_reduce([(da2_own[i] + da2_got[i].astype(F32)).astype(BF) for i in range(4)], "z")
    da2 = da2.astype(F32)
    dsecond = exchange(dsecond, PLANE)
    back_two, normed_two = norm_backward(middle, gain_two, da2)
    dmid = dm_own.astype(F32) + back_two
    da_own = dmid.astype(BF)
    da_two = jnp.concatenate([da_own, swap_core(da_own)], axis=0)
    do_msg = vmem_call(
        attended_grad_kernel, [((32, 32, 128), BF)], places, [da_two, out_matrix]
    )[0]
    do_got = lax.all_to_all(do_msg, ("yl", "x", "z"), split_axis=0, concat_axis=0, tiled=True)
    dout = vmem_call(
        out_grad_kernel,
        [((128, D), BF)] * 4,
        places,
        [o_two, tie(da_two, do_msg)],
        [((512, D), F32)],
    )
    dout = ring_reduce(dout, "z").reshape(16, 8, 2, 512).transpose(0, 2, 1, 3).reshape(16, 16, 512)
    dmsg = attend_backward(tables, (kv, query, mix, log_total), do_got, [])
    next_got = swap_core(tie(next_other, dmsg))
    next_sum = ring_reduce(
        [(next_own[i] + next_got[i].astype(F32)).astype(BF) for i in range(4)], "z"
    )
    final = middle + (next_sum.astype(F32) + proj_shift)
    dgot = lax.all_to_all(tie(dmsg, dsecond), ("yl", "x"), split_axis=0, concat_axis=0, tiled=True)

    here = (lax.broadcasted_iota(jnp.int32, (2, 4), 0) == core) & (
        lax.broadcasted_iota(jnp.int32, (2, 4), 1) == z_place
    )
    bias_rows = jnp.where(
        here[None, None, :, None, None, :, None],
        bias_sum[0].reshape(2, 2, 4, 8, 4).transpose(4, 0, 1, 2, 3)[:, :, None, :, :, None, :],
        0.0,
    ).reshape(4, 1024)
    sums = jnp.concatenate(
        [
            jnp.zeros((4, D), F32),
            jnp.stack(
                [
                    jnp.sum(da_own.astype(F32), axis=0),
                    jnp.sum(da2 * normed_two, axis=0),
                    jnp.sum(da2, axis=0),
                    jnp.sum(dm_own.astype(F32), axis=0),
                ]
            ),
            bias_rows,
            jnp.zeros((4, D), F32),
        ],
        axis=0,
    )
    da_one_own, da_one_other, dfirst = vmem_call(
        input_grad_kernel,
        [((4, 128, D), F32), ((4, 128, D), BF), ((16, 80, 512), BF)],
        places,
        [dgot, rows_z, rows_other, normed, qkv_matrix, sums, dout],
        [((16, D), F32), ((1024, 384), BF), ((1024, 512), BF)],
    )
    dfirst = exchange(dfirst, PLANE)
    da_one_swapped = swap_core(da_one_other)
    da_one = ring_reduce(
        [(da_one_own[i] + da_one_swapped[i].astype(F32)).astype(BF) for i in range(4)], "z"
    ).astype(F32)
    dfirst = jnp.sum(dfirst.astype(F32), axis=0) + 0.0 * da_one[0, 0]
    back_one, _ = norm_backward(own.astype(F32), rows[0], da_one)
    dtokens = dmid + back_one
    dsecond = jnp.sum(dsecond.astype(F32), axis=0)
    dproj = dsecond[64:].reshape(2, 32, 512).transpose(1, 0, 2).reshape(32, D)
    grad_out = dfirst[64:].reshape(2, 8, 512).transpose(1, 0, 2).reshape(8, D)

    back = jnp.concatenate(
        [dfirst[:64].astype(BF).reshape(8, 8, 512), dsecond[:64].astype(BF).reshape(8, 8, 512)], axis=2
    )
    back = lax.all_to_all(back, ("core", "z"), split_axis=0, concat_axis=0, tiled=True).astype(F32)
    kv_back = back[:, :, :256].reshape(2, 2, 2, 8, 2, 2, 64).transpose(3, 5, 1, 0, 2, 4, 6)
    q_back = back[:, :, 256:384].reshape(2, 2, 2, 8, 2, 64).transpose(3, 1, 0, 2, 4, 5)
    grad_qkv = jnp.concatenate([q_back.reshape(8, 1024), kv_back.reshape(8, 2048)], axis=1)
    grad_fc = (
        back[:, :, 512:]
        .reshape(2, 4, 8, 2, 2, 4, 32)
        .transpose(2, 3, 0, 4, 5, 1, 6)
        .reshape(8, 4096)
    )
    totals = jnp.sum(back[:, :, 384:396], axis=0)
    vecs = [totals[:, i][None] for i in range(8)]
    return (
        final.astype(BF)[None],
        dtokens[None],
        vecs[0],
        vecs[1],
        grad_qkv[None],
        vecs[2],
        vecs[3],
        grad_out[None],
        vecs[4],
        vecs[5],
        vecs[6],
        grad_fc[None],
        totals[:, 8:].reshape(1, 32),
        dproj[None],
        vecs[7],
    )


def solution(mesh):
    fine = Mesh(mesh.devices.reshape(2, 2, 2, 4, 4), AXES)
    dp, seq, every = ("yh", "core"), ("yl", "x", "z"), AXES
    vector, matrix, tokens = P(None, every), P(None, every, None), P(dp, seq, None)
    return jax.shard_map(
        on_device,
        mesh=fine,
        in_specs=(
            tokens,
            tokens,
            P(dp, None),
            P(dp, None),
            vector,
            vector,
            matrix,
            vector,
            vector,
            matrix,
            vector,
            vector,
            vector,
            matrix,
            vector,
            matrix,
            vector,
        ),
        out_specs=(
            tokens,
            tokens,
            vector,
            vector,
            matrix,
            vector,
            vector,
            matrix,
            vector,
            vector,
            vector,
            matrix,
            vector,
            matrix,
            vector,
        ),
        check_vma=False,
    )
```

```python
import functools

import jax
import jax.numpy as jnp
from jax import lax
from jax.experimental import pallas as pl
from jax.experimental.pallas import tpu as pltpu
from jax.sharding import Mesh, PartitionSpec as P

D = 1024
PIECE = 256
EPS = 1e-05
NEG = -1e30
LOG2E = 1.4426950408889634
BF = jnp.bfloat16
F32 = jnp.float32
AXES = ("yh", "core", "yl", "x", "z")
PLANE = ("yh", "yl", "x")
Y = ("yh", "yl")
QB = 512
KB = 1024


def plain_product(left_side, right_side):
    return jnp.dot(left_side, right_side, preferred_element_type=F32)


def left_product(left_side, right_side):
    return lax.dot_general(
        left_side, right_side, (((0,), (0,)), ((), ())), preferred_element_type=F32
    )


def right_product(left_side, right_side):
    return lax.dot_general(
        left_side, right_side, (((1,), (1,)), ((), ())), preferred_element_type=F32
    )


def layer_norm(values, gain, shift):
    center = values - jnp.mean(values, axis=-1, keepdims=True)
    spread = jnp.mean(center * center, axis=-1, keepdims=True)
    return center * lax.rsqrt(spread + EPS) * gain + shift


def norm_backward(values, gain, grad):
    center = values - jnp.mean(values, axis=-1, keepdims=True)
    spread = jnp.mean(center * center, axis=-1, keepdims=True)
    scale = lax.rsqrt(spread + EPS)
    normed = center * scale
    pulled = grad * gain
    back = scale * (
        pulled
        - jnp.mean(pulled, axis=-1, keepdims=True)
        - normed * jnp.mean(pulled * normed, axis=-1, keepdims=True)
    )
    return back, normed


def shift(values, axis, step):
    return lax.ppermute(values, axis, [(i, (i + step) % 4) for i in range(4)])


def swap_core(values):
    return lax.ppermute(values, "core", [(0, 1), (1, 0)])


def ring_blocks(values, axis):
    return [values, shift(values, axis, -1), shift(values, axis, 2), shift(values, axis, 1)]


def ring_stack(values, axis):
    return jnp.stack(ring_blocks(values, axis))


def add_all(terms):
    total = terms[0].astype(F32)
    for term in terms[1:]:
        total = total + term.astype(F32)
    return total.astype(BF)


def ring_reduce(blocks, axis):
    return add_all(ring_arrive(blocks, axis))


def ring_arrive(blocks, axis):
    return [
        blocks[0],
        shift(blocks[1], axis, 1),
        shift(blocks[2], axis, 2),
        shift(blocks[3], axis, -1),
    ]


def exchange(values, axes):
    return lax.all_to_all(values, axes, split_axis=0, concat_axis=0, tiled=True)


def spread_out(values, axes, count):
    return exchange(jnp.broadcast_to(values[None], (count,) + values.shape), axes)


def around(place, step):
    return lax.rem(place + step, 4)


def feature_row(y, side, x):
    return (y // 2) * 512 + side * 256 + (y % 2) * 128 + x * 32


def cost(microseconds):
    return pl.CostEstimate(
        flops=microseconds * 1_000_000_000, bytes_accessed=1, transcendentals=0
    )


def vmem_call(kernel, out_shape, places, arrays, scratch=(), after=(), microseconds=2):
    count = len(arrays)

    def body(*refs):
        kernel(*refs[: 1 + count], *refs[1 + count + len(after) :])

    return pl.pallas_call(
        body,
        out_shape=[jax.ShapeDtypeStruct(shape, dtype) for shape, dtype in out_shape],
        in_specs=[pl.BlockSpec(memory_space=pltpu.SMEM)]
        + [pl.BlockSpec(memory_space=pltpu.VMEM)] * count
        + [pl.BlockSpec(memory_space=pl.ANY)] * len(after),
        out_specs=[pl.BlockSpec(memory_space=pltpu.VMEM)] * len(out_shape),
        scratch_shapes=[pltpu.VMEM(shape, dtype) for shape, dtype in scratch],
        cost_estimate=cost(microseconds),
        compiler_params=pltpu.CompilerParams(vmem_limit_bytes=50 * 1024 * 1024),
    )(places, *arrays, *after)


def tie_kernel(*refs):
    pass


def tie(values, *after):
    return pl.pallas_call(
        tie_kernel,
        out_shape=jax.ShapeDtypeStruct(values.shape, values.dtype),
        in_specs=[pl.BlockSpec(memory_space=pl.ANY)] * (1 + len(after)),
        out_specs=pl.BlockSpec(memory_space=pl.ANY),
        input_output_aliases={0: 0},
    )(values, *after)


def lane_half(shape):
    return lax.broadcasted_iota(jnp.int32, shape, 1) < 64


def head_lanes(places):
    z, core = places[2], places[3]
    return pl.multiple_of((z // 2) * 512 + core * 256 + (z % 2) * 128, 128)


def qkv_kernel(places, source_weight, own, other, msg, normed, weight, rows):
    for chip in range(16):
        for side in range(2):
            row = feature_row(chip // 4, side, chip % 4)
            weight[row : row + 32, :] = source_weight[chip, side * 32 : side * 32 + 32, :]
    vectors = weight[:, 384:512].astype(F32)
    rows[...] = jnp.transpose(vectors)[0:16, :]
    gain, shift_row = rows[0:1, :], rows[1:2, :]
    lanes = pl.ds(head_lanes(places), 128)
    query_add = rows[2:3, lanes]
    value_add = jnp.broadcast_to(rows[3:4, lanes], (8, 128))
    left8 = lane_half((8, 128))
    first_add = jnp.where(left8, 0.0, pltpu.roll(value_add, 64, 1))[0:1]
    second_add = jnp.where(left8, 0.0, value_add)[0:1]
    left = lane_half((32, 128))
    for side, source in enumerate((own, other)):
        sequence = places[3] if side == 0 else 1 - places[3]
        for step in range(4):
            z = around(places[2], step)
            values = source[step].astype(F32)
            center = values - jnp.mean(values, axis=1, keepdims=True)
            spread = jnp.mean(center * center, axis=1, keepdims=True)
            row = (center * lax.rsqrt(spread + EPS) * gain + shift_row).astype(BF)
            normed[sequence, z] = row
            made = plain_product(row, weight[:, 0:384])
            pairs = (
                (made[:, 0:128] + first_add).astype(BF),
                (made[:, 128:256] + second_add).astype(BF),
            )
            query = made[:, 256:384] + query_add
            turned = pltpu.roll(query, 64, 1)
            begin = pl.multiple_of(z * 128, 128)
            q_begin = pl.multiple_of(512 + z * 32, 32)
            for part in range(2):
                top, bottom = part * 64, part * 64 + 32
                packed = (
                    jnp.where(left, query[top : top + 32], turned[bottom : bottom + 32]),
                    jnp.where(left, turned[top : top + 32], query[bottom : bottom + 32]),
                )
                for head in range(2):
                    task = sequence * 4 + head * 2 + part
                    msg[task, pl.ds(begin, 128), :] = pairs[head]
                    msg[task, pl.ds(q_begin, 32), :] = packed[head].astype(BF)


def out_kernel(places, got, b0, b1, b2, b3, own, other, attended, matrix):
    for up, ref in enumerate((b0, b1, b2, b3)):
        y = around(places[0], up)
        for turn in range(4):
            x = around(places[1], turn)
            row = pl.ds(pl.multiple_of((y * 4 + x) * 32, 32), 32)
            matrix[row, 0:512] = ref[turn, 128:160, :]
            matrix[row, 512:1024] = ref[turn, 160:192, :]
    left = lane_half((32, 128))
    for side in range(2):
        sequence = places[3] if side == 0 else 1 - places[3]
        for part in range(2):
            for pair in range(4):
                one = got[(sequence * 4 + part) * 4 + pair].astype(F32)
                two = got[(sequence * 4 + 2 + part) * 4 + pair].astype(F32)
                row = side * 128 + part * 64
                columns = slice(pair * 128, pair * 128 + 128)
                attended[row : row + 32, columns] = jnp.where(
                    left, one, pltpu.roll(two, 64, 1)
                ).astype(BF)
                attended[row + 32 : row + 64, columns] = jnp.where(
                    left, pltpu.roll(one, 64, 1), two
                ).astype(BF)
    product = plain_product(attended[...], matrix[...])
    own[...] = product[0:128]
    other[...] = product[128:256]


def feed_kernel(
    places,
    a2_own,
    a2_other,
    dm_own,
    dm_other,
    bias,
    w0,
    w1,
    w2,
    w3,
    next_own,
    next_other,
    da2_own,
    da2_other,
    sums,
    bias_sum,
    fc,
    proj,
    act_all,
    df_all,
):
    for up, weights in enumerate((w0, w1, w2, w3)):
        y = around(places[0], up)
        for turn in range(4):
            x = around(places[1], turn)
            for side in range(2):
                fc[pl.ds(pl.multiple_of(feature_row(y, side, x), 32), 32), :] = weights[
                    turn, side * 32 : side * 32 + 32, :
                ]
                proj[
                    pl.ds(pl.multiple_of((y * 4 + x) * 32, 32), 32),
                    side * 512 : side * 512 + 512,
                ] = weights[turn, 64 + side * 32 : 96 + side * 32, :]
    total = jnp.zeros((1, 512), F32)
    for half in range(4):
        a2, dm = (a2_own, dm_own) if half < 2 else (a2_other, dm_other)
        part = slice(half % 2 * 2, half % 2 * 2 + 2)
        pre = plain_product(a2[part].reshape(256, D), fc[...]) + bias[0:1, :]
        square = pre * pre
        bent = jnp.tanh(0.7978845608028654 * pre * (1.0 + 0.044715 * square))
        side = 0.5 * (1.0 + bent)
        act = (pre * side).astype(BF)
        slope = side + 0.5 * pre * (1.0 - bent * bent) * (
            0.7978845608028654 * (1.0 + 0.134145 * square)
        )
        df = (right_product(dm[part].reshape(256, D), proj[...]) * slope).astype(BF)
        rows = slice(half * 256, half * 256 + 256)
        act_all[rows] = act
        df_all[rows] = df
        total += jnp.sum(df.astype(F32), axis=0, keepdims=True)
        made = plain_product(act, proj[...]).reshape(2, 128, D)
        pulled = right_product(df, fc[...]).reshape(2, 128, D)
        if half < 2:
            next_own[part] = made
            da2_own[part] = pulled
        else:
            next_other[part] = made.astype(BF)
            da2_other[part] = pulled.astype(BF)
    bias_sum[...] = jnp.broadcast_to(total, (8, 512))
    fc_sum = left_product(a2_own[...].reshape(512, D), df_all[0:512]) + left_product(
        a2_other[...].reshape(512, D), df_all[512:1024]
    )
    proj_sum = left_product(act_all[0:512], dm_own[...].reshape(512, D)) + left_product(
        act_all[512:1024], dm_other[...].reshape(512, D)
    )
    for chip in range(16):
        for side in range(2):
            row = feature_row(chip // 4, side, chip % 4)
            sums[chip, side * 32 : side * 32 + 32, :] = fc_sum[row : row + 32].astype(BF)
            sums[chip, 64 + side * 32 : 96 + side * 32, :] = proj_sum[
                chip * 32 : chip * 32 + 32, side * 512 : side * 512 + 512
            ].astype(BF)


def attended_grad_kernel(places, da, matrix, msg):
    product = right_product(da[...], matrix[...])
    turned = [pltpu.roll(product[:, i * 128 : i * 128 + 128], 64, 1) for i in range(4)]
    left = lane_half((32, 128))
    for side in range(2):
        sequence = places[3] if side == 0 else 1 - places[3]
        for part in range(2):
            for pair in range(4):
                top = side * 128 + part * 64
                bottom = top + 32
                flat = product[:, pair * 128 : pair * 128 + 128]
                msg[(sequence * 4 + part) * 4 + pair] = jnp.where(
                    left, flat[top : top + 32], turned[pair][bottom : bottom + 32]
                ).astype(BF)
                msg[(sequence * 4 + 2 + part) * 4 + pair] = jnp.where(
                    left, turned[pair][top : top + 32], flat[bottom : bottom + 32]
                ).astype(BF)


def out_grad_kernel(places, attended, da, o0, o1, o2, o3, total):
    total[...] = left_product(attended[...], da[...])
    for step, ref in enumerate((o0, o1, o2, o3)):
        z = around(places[2], step)
        ref[...] = jnp.concatenate(
            [total[pl.ds(pl.multiple_of(chip * 32 + z * 8, 8), 8), :] for chip in range(16)], axis=0
        ).astype(BF)


def input_grad_kernel(
    places, got, own, other, normed, weight, sums, dout, da_own, da_other, weight_sum, rows, dqkv, total
):
    left = lane_half((32, 128))
    for sequence in range(2):
        for head in range(2):
            task = (sequence * 2 + head) * 2
            dqkv[sequence * 512 : sequence * 512 + 512, head * 128 : head * 128 + 128] = (
                got[task, 0:512, :].astype(F32) + got[task + 1, 0:512, :].astype(F32)
            ).astype(BF)
        for part in range(2):
            for z in range(4):
                at = slice(512 + z * 32, 544 + z * 32)
                one = got[sequence * 4 + part, at, :].astype(F32)
                two = got[sequence * 4 + 2 + part, at, :].astype(F32)
                row = sequence * 512 + z * 128 + part * 64
                dqkv[row : row + 32, 256:384] = jnp.where(
                    left, one, pltpu.roll(two, 64, 1)
                ).astype(BF)
                dqkv[row + 32 : row + 64, 256:384] = jnp.where(
                    left, pltpu.roll(one, 64, 1), two
                ).astype(BF)
    column = jnp.sum(dqkv[...].astype(F32), axis=0, keepdims=True)
    column = jnp.broadcast_to(column, (8, 384))
    left8 = lane_half((8, 128))
    value_sum = jnp.where(left8, pltpu.roll(column[:, 0:128], 64, 1), column[:, 128:256])
    gain_sum = jnp.zeros((1, D), F32)
    shift_sum = jnp.zeros((1, D), F32)
    for side, source in enumerate((own, other)):
        sequence = places[3] if side == 0 else 1 - places[3]
        for step in range(4):
            z = around(places[2], step)
            begin = pl.multiple_of(sequence * 512 + z * 128, 128)
            grad = right_product(dqkv[pl.ds(begin, 128), :], weight[:, 0:384])
            values = source[step].astype(F32)
            center = values - jnp.mean(values, axis=1, keepdims=True)
            spread = jnp.mean(center * center, axis=1, keepdims=True)
            gain_sum += jnp.sum(grad * (center * lax.rsqrt(spread + EPS)), axis=0, keepdims=True)
            shift_sum += jnp.sum(grad, axis=0, keepdims=True)
            if side == 0:
                da_own[step] = grad
            else:
                da_other[step] = grad.astype(BF)
    rows[...] = sums[...]
    rows[0:1, :] = gain_sum
    rows[1:2, :] = shift_sum
    lanes = pl.ds(head_lanes(places), 128)
    rows[2:4, :] = jnp.zeros((2, D), F32)
    rows[2:3, lanes] = column[0:1, 256:384]
    rows[3:4, lanes] = value_sum[0:1]
    total[:, 0:384] = left_product(normed[...].reshape(1024, D), dqkv[...]).astype(BF)
    total[:, 384:512] = jnp.transpose(
        jnp.concatenate([rows[...], jnp.zeros((112, D), F32)], axis=0)
    ).astype(BF)
    for chip in range(16):
        for side in range(2):
            row = feature_row(chip // 4, side, chip % 4)
            weight_sum[chip, side * 32 : side * 32 + 32, :] = total[row : row + 32, :]
        weight_sum[chip, 64:80, :] = dout[chip]


def limit_of(position, starts):
    limit = position
    for start in starts:
        limit = jnp.where((position >= start) & (position < start + PIECE), start + PIECE - 1, limit)
    return limit


def over_blocks(step, full, count, carry):
    carry = lax.fori_loop(0, full, functools.partial(step, False), carry)
    return lax.fori_loop(full, count, functools.partial(step, True), carry)


def forward_kernel(order_ref, source_ref, where_ref, starts_ref, got_ref, *refs):
    kv_ref, q_ref, o_ref, lse_ref, msg_ref, one_ref = refs[-6:]
    starts = [starts_ref[i] for i in range(6)]
    wide = lane_half((64, 128))
    left = lane_half((32, 128))

    @pl.loop(0, 8)
    def _(group):
        for i in range(8):
            stored = order_ref[group * 8 + i]
            block = got_ref[
                stored // 8, pl.ds(pl.multiple_of((stored % 8) * 64, 64), 64), :
            ]
            at = pl.ds(pl.multiple_of(group * 512 + i * 64, 64), 64)
            kv_ref[at, :] = block
            one_ref[at, :] = jnp.where(wide, jnp.ones_like(block), block)

    @pl.loop(0, 4)
    def _(group):
        for i in range(8):
            source = source_ref[group * 8 + i]
            packed = got_ref[
                source // 4, pl.ds(pl.multiple_of(512 + (source % 4) * 32, 32), 32), :
            ].astype(F32) * 0.125
            row = pl.multiple_of(group * 512 + i * 64, 64)
            q_ref[pl.ds(row, 32), :] = jnp.where(left, packed, 0.0).astype(BF)
            q_ref[pl.ds(row + 32, 32), :] = jnp.where(
                left, pltpu.roll(packed, 64, 1), 0.0
            ).astype(BF)

    @pl.loop(0, 2048 // QB)
    def _(block):
        row = pl.multiple_of(block * QB, QB)
        query = q_ref[pl.ds(row, QB), :]
        spans = QB // 64
        first = limit_of(where_ref[block * spans] * 64, starts)
        last = limit_of(where_ref[block * spans + spans - 1] * 64 + 63, starts)
        full = (first + 1) // KB
        count = last // KB + 1
        inner = lax.broadcasted_iota(jnp.int32, (64, 1), 0)
        position = jnp.concatenate(
            [where_ref[block * spans + i] * 64 + inner for i in range(spans)], axis=0
        )
        limit = limit_of(position, starts)

        def scores_of(masked, index):
            begin = pl.multiple_of(index * KB, KB)
            scores = right_product(query, kv_ref[pl.ds(begin, KB), :])
            if masked:
                key_pos = begin + lax.broadcasted_iota(jnp.int32, (1, KB), 1)
                scores = jnp.where(key_pos <= limit, scores, NEG)
            return scores

        def highest(masked, index, high):
            scores = scores_of(masked, index)
            for i in range(KB // 128):
                high = jnp.maximum(high, scores[:, i * 128 : i * 128 + 128])
            return high

        def mixture(masked, index, total):
            begin = pl.multiple_of(index * KB, KB)
            raised = jnp.exp2((scores_of(masked, index) - maxima) * LOG2E)
            return total + plain_product(raised.astype(BF), one_ref[pl.ds(begin, KB), :])

        high = over_blocks(highest, full, count, jnp.full((QB, 128), NEG, F32))
        maxima = jnp.max(high, axis=1, keepdims=True)
        total = over_blocks(mixture, full, count, jnp.zeros((QB, 128), F32))
        attended = total / pltpu.roll(total, 64, 1)
        o_ref[pl.ds(row, QB), :] = jnp.where(lane_half((QB, 128)), 0.0, attended).astype(BF)
        log_total = maxima * LOG2E + jnp.log2(total[:, 0:1])
        lse_ref[block] = jnp.transpose(jnp.broadcast_to(log_total, (QB, 128)))[0:8, :]
        turned = pltpu.roll(attended, 64, 1)
        for i in range(spans):
            top, bottom = turned[i * 64 : i * 64 + 32], attended[i * 64 + 32 : i * 64 + 64]
            msg_ref[source_ref[block * spans + i]] = jnp.where(left, top, bottom).astype(BF)


def backward_kernel(
    order_ref,
    source_ref,
    where_ref,
    starts_ref,
    kv_ref,
    q_ref,
    o_ref,
    lse_ref,
    got_ref,
    *refs,
):
    msg_ref, do_ref, sum_ref = refs[-3:]
    starts = [starts_ref[i] for i in range(6)]

    left = lane_half((32, 128))

    @pl.loop(0, 4)
    def _(group):
        for i in range(8):
            packed = got_ref[source_ref[group * 8 + i]].astype(F32)
            row = pl.multiple_of(group * 512 + i * 64, 64)
            do_ref[pl.ds(row, 32), :] = jnp.where(left, 0.0, pltpu.roll(packed, 64, 1)).astype(BF)
            do_ref[pl.ds(row + 32, 32), :] = jnp.where(left, 0.0, packed).astype(BF)

    sum_ref[...] = jnp.zeros_like(sum_ref)

    @pl.loop(0, 2048 // QB)
    def _(block):
        row = pl.multiple_of(block * QB, QB)
        query = q_ref[pl.ds(row, QB), :]
        grad = do_ref[pl.ds(row, QB), :]
        both = jnp.concatenate([query, grad], axis=0)
        spans = QB // 64
        first = limit_of(where_ref[block * spans] * 64, starts)
        last = limit_of(where_ref[block * spans + spans - 1] * 64 + 63, starts)
        full = (first + 1) // KB
        count = last // KB + 1
        inner = lax.broadcasted_iota(jnp.int32, (1, 64), 1)
        position = jnp.concatenate(
            [where_ref[block * spans + i] * 64 + inner for i in range(spans)], axis=1
        )
        limit = limit_of(position, starts)
        log_total = lse_ref[block][0:1, :]
        product = grad.astype(F32) * o_ref[pl.ds(row, QB), :].astype(F32)
        delta = lax.dot_general(
            jnp.ones((8, 128), F32),
            product,
            (((1,), (1,)), ((), ())),
            precision=lax.Precision.HIGHEST,
            preferred_element_type=F32,
        )[0:1, :]

        def step(masked, index, total):
            begin = pl.multiple_of(index * KB, KB)
            pair = kv_ref[pl.ds(begin, KB), :]
            scores = right_product(pair, query)
            if masked:
                key_pos = begin + lax.broadcasted_iota(jnp.int32, (KB, 1), 0)
                scores = jnp.where(key_pos <= limit, scores, NEG)
            weights = jnp.exp2(scores * LOG2E - log_total)
            grad_scores = (weights * (right_product(pair, grad) - delta)).astype(BF)
            sum_ref[pl.ds(begin, KB), :] += plain_product(
                jnp.concatenate([grad_scores, weights.astype(BF)], axis=1), both
            )
            return total + left_product(grad_scores, pair)

        total = over_blocks(step, full, count, jnp.zeros((QB, 128), F32)) * 0.125
        turned = pltpu.roll(total, 64, 1)
        for i in range(spans):
            top, bottom = total[i * 64 : i * 64 + 32], turned[i * 64 + 32 : i * 64 + 64]
            source = source_ref[block * spans + i]
            msg_ref[
                source // 4, pl.ds(pl.multiple_of(512 + (source % 4) * 32, 32), 32), :
            ] = jnp.where(lane_half(top.shape), top, bottom).astype(BF)

    @pl.loop(0, 8)
    def _(group):
        for i in range(8):
            stored = order_ref[group * 8 + i]
            msg_ref[stored // 8, pl.ds(pl.multiple_of((stored % 8) * 64, 64), 64), :] = sum_ref[
                pl.ds(pl.multiple_of(group * 512 + i * 64, 64), 64), :
            ].astype(BF)


def attend_forward(tables, got, after):
    shapes = [
        jax.ShapeDtypeStruct((4096, 128), BF),
        jax.ShapeDtypeStruct((2048, 128), BF),
        jax.ShapeDtypeStruct((2048, 128), BF),
        jax.ShapeDtypeStruct((2048 // QB, 8, QB), F32),
        jax.ShapeDtypeStruct((32, 32, 128), BF),
    ]
    return pl.pallas_call(
        forward_kernel,
        out_shape=shapes,
        in_specs=[pl.BlockSpec(memory_space=pltpu.SMEM)] * 4
        + [pl.BlockSpec(memory_space=pltpu.VMEM)]
        + [pl.BlockSpec(memory_space=pl.ANY)] * len(after),
        out_specs=[pl.BlockSpec(memory_space=pltpu.VMEM)] * 5,
        scratch_shapes=[pltpu.VMEM((4096, 128), BF)],
        cost_estimate=cost(25),
        compiler_params=pltpu.CompilerParams(vmem_limit_bytes=48 * 1024 * 1024),
    )(*tables, got, *after)


def attend_backward(tables, saved, got, after):
    return pl.pallas_call(
        backward_kernel,
        out_shape=jax.ShapeDtypeStruct((8, 640, 128), BF),
        in_specs=[pl.BlockSpec(memory_space=pltpu.SMEM)] * 4
        + [pl.BlockSpec(memory_space=pltpu.VMEM)] * 5
        + [pl.BlockSpec(memory_space=pl.ANY)] * len(after),
        out_specs=pl.BlockSpec(memory_space=pltpu.VMEM),
        scratch_shapes=[pltpu.VMEM((2048, 128), BF), pltpu.VMEM((4096, 128), F32)],
        cost_estimate=cost(25),
        compiler_params=pltpu.CompilerParams(vmem_limit_bytes=48 * 1024 * 1024),
    )(*tables, *saved, got, *after)


def order_tables(span_order, piece_starts, part):
    places = jnp.arange(64, dtype=jnp.int32)
    order = jnp.sum(jnp.where(span_order[None, :] == places[:, None], places[None, :], 0), axis=1)
    mine = lax.dynamic_index_in_dim(span_order.reshape(32, 2), part, 1, keepdims=False)
    rank = jnp.sum((mine[None, :] < mine[:, None]).astype(jnp.int32), axis=1)
    sources = jnp.arange(32, dtype=jnp.int32)
    hit = rank[None, :] == sources[:, None]
    source = jnp.sum(jnp.where(hit, sources[None, :], 0), axis=1)
    where = jnp.sum(jnp.where(hit, mine[None, :], 0), axis=1)
    return order.astype(jnp.int32), source.astype(jnp.int32), where.astype(jnp.int32), piece_starts


def on_device(
    tokens,
    out_grad,
    piece_starts,
    span_order,
    ln1_gain,
    ln1_bias,
    qkv_weight,
    query_bias,
    value_bias,
    out_weight,
    out_bias,
    ln2_gain,
    ln2_bias,
    fc_weight,
    fc_bias,
    proj_weight,
    proj_bias,
):
    core = lax.axis_index("core")
    z_place = lax.axis_index("z")
    x_place = lax.axis_index("x")
    y_place = lax.axis_index(Y)
    sequence = lax.axis_index("yl")
    head_part = x_place // 2
    query_part = x_place % 2
    places = jnp.stack([y_place, x_place, z_place, core]).astype(jnp.int32)
    own = tokens[0]
    dm_own = out_grad[0]

    both_tables = lax.all_gather(
        jnp.concatenate([span_order[0], piece_starts[0]]), "core", axis=0, tiled=False
    )
    table = lax.dynamic_index_in_dim(both_tables, sequence, 0, keepdims=False)
    tables = order_tables(table[:64], table[64:], query_part)

    qkv_parts = qkv_weight[0].reshape(8, 3, 2, 2, 2, 2, 64)
    kv_cols = qkv_parts[:, 1:].transpose(3, 2, 4, 0, 5, 1, 6).reshape(2, 4, 8, 256)
    q_cols = qkv_parts[:, 0].transpose(2, 1, 3, 0, 4, 5).reshape(2, 4, 8, 128)
    fc_cols = (
        fc_weight[0]
        .reshape(8, 2, 2, 2, 4, 4, 32)
        .transpose(2, 5, 0, 1, 3, 4, 6)
        .reshape(2, 4, 8, 512)
    )
    members = (
        ln1_gain,
        ln1_bias,
        query_bias,
        value_bias,
        out_bias,
        ln2_gain,
        ln2_bias,
        proj_bias,
    )
    row_index = lax.broadcasted_iota(jnp.int32, (8, 8), 0)
    vectors = jnp.zeros((8, 8), BF)
    for i, member in enumerate(members):
        vectors = jnp.where(row_index == i, member, vectors)
    vectors = jnp.concatenate(
        [
            vectors.T,
            jnp.zeros((8, 24), BF),
            jnp.pad(fc_bias, ((0, 7), (0, 0))),
            jnp.zeros((8, 64), BF),
        ],
        axis=1,
    )
    vec_cols = jnp.broadcast_to(vectors[None, None], (2, 4, 8, 128))
    packed = jnp.concatenate([kv_cols, q_cols, vec_cols, fc_cols], axis=3)
    packed = packed.reshape(8, 8, 1024)
    rows_z = ring_blocks(own, "z")
    spread = exchange(packed, ("core", "z"))


    dm_z = ring_blocks(tie(jnp.concatenate([dm_own, out_weight[0]], axis=0), spread), "z")
    out_rows = jnp.stack([block[128:] for block in dm_z])
    out_rows = jnp.roll(out_rows, z_place, axis=0).reshape(32, 2, 512)
    out_rows = out_rows.transpose(1, 0, 2).reshape(64, 512)
    dm_z = jnp.stack([block[:128] for block in dm_z])
    dm_other = swap_core(dm_z)

    first = spread_out(spread[:, :, :512].reshape(64, 512), PLANE, 16)
    proj_halves = proj_weight[0].reshape(32, 2, 512).transpose(1, 0, 2).reshape(64, 512)
    second = jnp.concatenate([spread[:, :, 512:].reshape(64, 512), proj_halves, out_rows], axis=0)
    second = ring_blocks(ring_stack(second, "x"), Y)
    rows_z = jnp.stack(rows_z)
    rows_other = swap_core(rows_z)

    msg, normed, qkv_matrix, rows = vmem_call(
        qkv_kernel,
        [
            ((8, 640, 128), BF),
            ((2, 4, 128, D), BF),
            ((1024, 512), BF),
            ((16, D), F32),
        ],
        places,
        [first, rows_z, rows_other],
        microseconds=5,
    )
    got = lax.all_to_all(msg, ("yl", "x"), split_axis=0, concat_axis=0, tiled=True)
    kv, query, mix, log_total, o_msg = attend_forward(
        tables, got, []
    )
    o_got = lax.all_to_all(o_msg, ("yl", "x", "z"), split_axis=0, concat_axis=0, tiled=True)
    out_shift, gain_two, shift_two, proj_shift = [rows[i] for i in range(4, 8)]
    part_own, part_other, o_two, out_matrix = vmem_call(
        out_kernel,
        [((128, D), F32), ((128, D), F32), ((256, 512), BF), ((512, D), BF)],
        places,
        [o_got, *second],
    )
    middle = own.astype(F32) + (part_own + swap_core(part_other) + out_shift)
    a2_own = layer_norm(middle, gain_two, shift_two).astype(BF)
    a2_z = ring_stack(a2_own, "z")
    fc_shift = qkv_matrix.reshape(2, 2, 2, 4, 4, 8, 512)[:, :, :, :, :, 0, 416:448]
    fc_shift = lax.dynamic_index_in_dim(fc_shift, core, 1, keepdims=False)
    fc_shift = lax.dynamic_index_in_dim(fc_shift, z_place, 3, keepdims=False)
    fc_shift = jnp.broadcast_to(fc_shift.reshape(1, 512).astype(F32), (8, 512))
    a2_other = swap_core(a2_z)
    next_own, next_other, da2_own, da2_other, dsecond, bias_sum = vmem_call(
        feed_kernel,
        [
            ((4, 128, D), F32),
            ((4, 128, D), BF),
            ((4, 128, D), F32),
            ((4, 128, D), BF),
            ((16, 128, 512), BF),
            ((8, 512), F32),
        ],
        places,
        [a2_z, a2_other, dm_z, dm_other, fc_shift, *second],
        [((1024, 512), BF), ((512, D), BF), ((1024, 512), BF), ((1024, 512), BF)],
        microseconds=12,
    )
    da2_got = swap_core(da2_other)
    da2 = ring_reduce([(da2_own[i] + da2_got[i].astype(F32)).astype(BF) for i in range(4)], "z")
    da2 = da2.astype(F32)
    back_two, normed_two = norm_backward(middle, gain_two, da2)
    dmid = dm_own.astype(F32) + back_two
    da_own = dmid.astype(BF)
    da_two = jnp.concatenate([da_own, swap_core(da_own)], axis=0)
    do_msg = vmem_call(
        attended_grad_kernel, [((32, 32, 128), BF)], places, [da_two, out_matrix]
    )[0]
    do_got = lax.all_to_all(do_msg, ("yl", "x", "z"), split_axis=0, concat_axis=0, tiled=True)
    next_got = swap_core(tie(next_other, do_msg))
    next_parts = [(next_own[i] + next_got[i].astype(F32)).astype(BF) for i in range(4)]
    next_sum = ring_arrive(next_parts, "z")
    final = middle + (add_all(next_sum).astype(F32) + proj_shift)
    dsecond = exchange(tie(dsecond, do_got), PLANE)
    dmsg = attend_backward(tables, (kv, query, mix, log_total), do_got, next_parts[1:])
    dout = vmem_call(
        out_grad_kernel,
        [((128, D), BF)] * 4,
        places,
        [o_two, tie(da_two, dmsg)],
        [((512, D), F32)],
    )
    dout = ring_arrive(dout, "z")
    dout = add_all(dout).reshape(16, 8, 2, 512).transpose(0, 2, 1, 3).reshape(16, 16, 512)
    dgot = exchange(tie(dmsg, dsecond, *next_sum[1:]), ("yl", "x"))

    here = (lax.broadcasted_iota(jnp.int32, (2, 4), 0) == core) & (
        lax.broadcasted_iota(jnp.int32, (2, 4), 1) == z_place
    )
    bias_rows = jnp.where(
        here[None, None, :, None, None, :, None],
        bias_sum[0].reshape(2, 2, 4, 8, 4).transpose(4, 0, 1, 2, 3)[:, :, None, :, :, None, :],
        0.0,
    ).reshape(4, 1024)
    sums = jnp.concatenate(
        [
            jnp.zeros((4, D), F32),
            jnp.stack(
                [
                    jnp.sum(da_own.astype(F32), axis=0),
                    jnp.sum(da2 * normed_two, axis=0),
                    jnp.sum(da2, axis=0),
                    jnp.sum(dm_own.astype(F32), axis=0),
                ]
            ),
            bias_rows,
            jnp.zeros((4, D), F32),
        ],
        axis=0,
    )
    da_one_own, da_one_other, dfirst = vmem_call(
        input_grad_kernel,
        [((4, 128, D), F32), ((4, 128, D), BF), ((16, 80, 512), BF)],
        places,
        [dgot, rows_z, rows_other, normed, qkv_matrix, sums, dout],
        [((16, D), F32), ((1024, 384), BF), ((1024, 512), BF)],
        microseconds=8,
    )
    dfirst = exchange(dfirst, PLANE)
    da_one_swapped = swap_core(da_one_other)
    da_one = ring_reduce(
        [(da_one_own[i] + da_one_swapped[i].astype(F32)).astype(BF) for i in range(4)], "z"
    ).astype(F32)
    dfirst = jnp.sum(dfirst.astype(F32), axis=0) + 0.0 * da_one[0, 0]
    back_one, _ = norm_backward(own.astype(F32), rows[0], da_one)
    dtokens = dmid + back_one
    dsecond = jnp.sum(dsecond.astype(F32), axis=0)
    dproj = dsecond[64:].reshape(2, 32, 512).transpose(1, 0, 2).reshape(32, D)
    grad_out = dfirst[64:].reshape(2, 8, 512).transpose(1, 0, 2).reshape(8, D)

    back = jnp.concatenate(
        [dfirst[:64].astype(BF).reshape(8, 8, 512), dsecond[:64].astype(BF).reshape(8, 8, 512)], axis=2
    )
    back = lax.all_to_all(back, ("core", "z"), split_axis=0, concat_axis=0, tiled=True).astype(F32)
    kv_back = back[:, :, :256].reshape(2, 2, 2, 8, 2, 2, 64).transpose(3, 5, 1, 0, 2, 4, 6)
    q_back = back[:, :, 256:384].reshape(2, 2, 2, 8, 2, 64).transpose(3, 1, 0, 2, 4, 5)
    grad_qkv = jnp.concatenate([q_back.reshape(8, 1024), kv_back.reshape(8, 2048)], axis=1)
    grad_fc = (
        back[:, :, 512:]
        .reshape(2, 4, 8, 2, 2, 4, 32)
        .transpose(2, 3, 0, 4, 5, 1, 6)
        .reshape(8, 4096)
    )
    totals = jnp.sum(back[:, :, 384:396], axis=0)
    vecs = [totals[:, i][None] for i in range(8)]
    return (
        final.astype(BF)[None],
        dtokens[None],
        vecs[0],
        vecs[1],
        grad_qkv[None],
        vecs[2],
        vecs[3],
        grad_out[None],
        vecs[4],
        vecs[5],
        vecs[6],
        grad_fc[None],
        totals[:, 8:].reshape(1, 32),
        dproj[None],
        vecs[7],
    )


def solution(mesh):
    fine = Mesh(mesh.devices.reshape(2, 2, 2, 4, 4), AXES)
    dp, seq, every = ("yh", "core"), ("yl", "x", "z"), AXES
    vector, matrix, tokens = P(None, every), P(None, every, None), P(dp, seq, None)
    return jax.shard_map(
        on_device,
        mesh=fine,
        in_specs=(
            tokens,
            tokens,
            P(dp, None),
            P(dp, None),
            vector,
            vector,
            matrix,
            vector,
            vector,
            matrix,
            vector,
            vector,
            vector,
            matrix,
            vector,
            matrix,
            vector,
        ),
        out_specs=(
            tokens,
            tokens,
            vector,
            vector,
            matrix,
            vector,
            vector,
            matrix,
            vector,
            vector,
            vector,
            matrix,
            vector,
            matrix,
            vector,
        ),
        check_vma=False,
    )
```

```python
import functools

import jax
import jax.numpy as jnp
from jax import lax
from jax.experimental import pallas as pl
from jax.experimental.pallas import tpu as pltpu
from jax.sharding import Mesh, PartitionSpec as P

D = 1024
PIECE = 256
EPS = 1e-05
NEG = -1e30
LOG2E = 1.4426950408889634
BF = jnp.bfloat16
F32 = jnp.float32
AXES = ("yh", "core", "yl", "x", "z")
PLANE = ("yh", "yl", "x")
Y = ("yh", "yl")
QB = 512
KB = 1024


def plain_product(left_side, right_side):
    return jnp.dot(left_side, right_side, preferred_element_type=F32)


def left_product(left_side, right_side):
    return lax.dot_general(
        left_side, right_side, (((0,), (0,)), ((), ())), preferred_element_type=F32
    )


def right_product(left_side, right_side):
    return lax.dot_general(
        left_side, right_side, (((1,), (1,)), ((), ())), preferred_element_type=F32
    )


def layer_norm(values, gain, shift):
    center = values - jnp.mean(values, axis=-1, keepdims=True)
    spread = jnp.mean(center * center, axis=-1, keepdims=True)
    return center * lax.rsqrt(spread + EPS) * gain + shift


def norm_backward(values, gain, grad):
    center = values - jnp.mean(values, axis=-1, keepdims=True)
    spread = jnp.mean(center * center, axis=-1, keepdims=True)
    scale = lax.rsqrt(spread + EPS)
    normed = center * scale
    pulled = grad * gain
    back = scale * (
        pulled
        - jnp.mean(pulled, axis=-1, keepdims=True)
        - normed * jnp.mean(pulled * normed, axis=-1, keepdims=True)
    )
    return back, normed


def shift(values, axis, step):
    return lax.ppermute(values, axis, [(i, (i + step) % 4) for i in range(4)])


def swap_core(values):
    return lax.ppermute(values, "core", [(0, 1), (1, 0)])


def ring_blocks(values, axis):
    return [values, shift(values, axis, -1), shift(values, axis, 2), shift(values, axis, 1)]


def ring_stack(values, axis):
    return jnp.stack(ring_blocks(values, axis))


def add_all(terms):
    total = terms[0].astype(F32)
    for term in terms[1:]:
        total = total + term.astype(F32)
    return total.astype(BF)


def ring_reduce(blocks, axis):
    return add_all(ring_arrive(blocks, axis))


def ring_arrive(blocks, axis):
    return [
        blocks[0],
        shift(blocks[1], axis, 1),
        shift(blocks[2], axis, 2),
        shift(blocks[3], axis, -1),
    ]


def exchange(values, axes):
    return lax.all_to_all(values, axes, split_axis=0, concat_axis=0, tiled=True)


def spread_out(values, axes, count):
    return exchange(jnp.broadcast_to(values[None], (count,) + values.shape), axes)


def around(place, step):
    return lax.rem(place + step, 4)


def feature_row(y, side, x):
    return (y // 2) * 512 + side * 256 + (y % 2) * 128 + x * 32


def cost(microseconds):
    return pl.CostEstimate(
        flops=microseconds * 1_000_000_000, bytes_accessed=1, transcendentals=0
    )


def vmem_call(kernel, out_shape, places, arrays, scratch=(), after=(), microseconds=2):
    count = len(arrays)

    def body(*refs):
        kernel(*refs[: 1 + count], *refs[1 + count + len(after) :])

    return pl.pallas_call(
        body,
        out_shape=[jax.ShapeDtypeStruct(shape, dtype) for shape, dtype in out_shape],
        in_specs=[pl.BlockSpec(memory_space=pltpu.SMEM)]
        + [pl.BlockSpec(memory_space=pltpu.VMEM)] * count
        + [pl.BlockSpec(memory_space=pl.ANY)] * len(after),
        out_specs=[pl.BlockSpec(memory_space=pltpu.VMEM)] * len(out_shape),
        scratch_shapes=[pltpu.VMEM(shape, dtype) for shape, dtype in scratch],
        cost_estimate=cost(microseconds),
        compiler_params=pltpu.CompilerParams(vmem_limit_bytes=50 * 1024 * 1024),
    )(places, *arrays, *after)


def tie_kernel(*refs):
    pass


def tie(values, *after):
    return pl.pallas_call(
        tie_kernel,
        out_shape=jax.ShapeDtypeStruct(values.shape, values.dtype),
        in_specs=[pl.BlockSpec(memory_space=pl.ANY)] * (1 + len(after)),
        out_specs=pl.BlockSpec(memory_space=pl.ANY),
        input_output_aliases={0: 0},
    )(values, *after)


def lane_half(shape):
    return lax.broadcasted_iota(jnp.int32, shape, 1) < 64


def head_lanes(places):
    z, core = places[2], places[3]
    return pl.multiple_of((z // 2) * 512 + core * 256 + (z % 2) * 128, 128)


def qkv_kernel(places, source_weight, own, other, msg, normed, weight, rows):
    for chip in range(16):
        for side in range(2):
            row = feature_row(chip // 4, side, chip % 4)
            weight[row : row + 32, :] = source_weight[chip, side * 32 : side * 32 + 32, :]
    vectors = weight[:, 384:512].astype(F32)
    rows[...] = jnp.transpose(vectors)[0:16, :]
    gain, shift_row = rows[0:1, :], rows[1:2, :]
    lanes = pl.ds(head_lanes(places), 128)
    query_add = rows[2:3, lanes]
    value_add = jnp.broadcast_to(rows[3:4, lanes], (8, 128))
    left8 = lane_half((8, 128))
    first_add = jnp.where(left8, 0.0, pltpu.roll(value_add, 64, 1))[0:1]
    second_add = jnp.where(left8, 0.0, value_add)[0:1]
    left = lane_half((32, 128))
    for side, source in enumerate((own, other)):
        sequence = places[3] if side == 0 else 1 - places[3]
        for step in range(4):
            z = around(places[2], step)
            values = source[step].astype(F32)
            center = values - jnp.mean(values, axis=1, keepdims=True)
            spread = jnp.mean(center * center, axis=1, keepdims=True)
            row = (center * lax.rsqrt(spread + EPS) * gain + shift_row).astype(BF)
            normed[sequence, z] = row
            made = plain_product(row, weight[:, 0:384])
            pairs = (
                (made[:, 0:128] + first_add).astype(BF),
                (made[:, 128:256] + second_add).astype(BF),
            )
            query = made[:, 256:384] + query_add
            turned = pltpu.roll(query, 64, 1)
            begin = pl.multiple_of(z * 128, 128)
            q_begin = pl.multiple_of(512 + z * 32, 32)
            for part in range(2):
                top, bottom = part * 64, part * 64 + 32
                packed = (
                    jnp.where(left, query[top : top + 32], turned[bottom : bottom + 32]),
                    jnp.where(left, turned[top : top + 32], query[bottom : bottom + 32]),
                )
                for head in range(2):
                    task = sequence * 4 + head * 2 + part
                    msg[task, pl.ds(begin, 128), :] = pairs[head]
                    msg[task, pl.ds(q_begin, 32), :] = packed[head].astype(BF)


def out_kernel(places, got, b0, b1, b2, b3, own, other, attended, matrix):
    for up, ref in enumerate((b0, b1, b2, b3)):
        y = around(places[0], up)
        for turn in range(4):
            x = around(places[1], turn)
            row = pl.ds(pl.multiple_of((y * 4 + x) * 32, 32), 32)
            matrix[row, 0:512] = ref[turn, 128:160, :]
            matrix[row, 512:1024] = ref[turn, 160:192, :]
    left = lane_half((32, 128))
    for side in range(2):
        sequence = places[3] if side == 0 else 1 - places[3]
        for part in range(2):
            for pair in range(4):
                one = got[(sequence * 4 + part) * 4 + pair].astype(F32)
                two = got[(sequence * 4 + 2 + part) * 4 + pair].astype(F32)
                row = side * 128 + part * 64
                columns = slice(pair * 128, pair * 128 + 128)
                attended[row : row + 32, columns] = jnp.where(
                    left, one, pltpu.roll(two, 64, 1)
                ).astype(BF)
                attended[row + 32 : row + 64, columns] = jnp.where(
                    left, pltpu.roll(one, 64, 1), two
                ).astype(BF)
    product = plain_product(attended[...], matrix[...])
    own[...] = product[0:128]
    other[...] = product[128:256]


def feed_kernel(
    places,
    a2_own,
    a2_other,
    dm_own,
    dm_other,
    bias,
    w0,
    w1,
    w2,
    w3,
    next_own,
    next_other,
    da2_own,
    da2_other,
    sums,
    bias_sum,
    fc,
    proj,
    act_all,
    df_all,
):
    for up, weights in enumerate((w0, w1, w2, w3)):
        y = around(places[0], up)
        for turn in range(4):
            x = around(places[1], turn)
            for side in range(2):
                fc[pl.ds(pl.multiple_of(feature_row(y, side, x), 32), 32), :] = weights[
                    turn, side * 32 : side * 32 + 32, :
                ]
                proj[
                    pl.ds(pl.multiple_of((y * 4 + x) * 32, 32), 32),
                    side * 512 : side * 512 + 512,
                ] = weights[turn, 64 + side * 32 : 96 + side * 32, :]
    total = jnp.zeros((1, 512), F32)
    for half in range(4):
        a2, dm = (a2_own, dm_own) if half < 2 else (a2_other, dm_other)
        part = slice(half % 2 * 2, half % 2 * 2 + 2)
        pre = plain_product(a2[part].reshape(256, D), fc[...]) + bias[0:1, :]
        square = pre * pre
        bent = jnp.tanh(0.7978845608028654 * pre * (1.0 + 0.044715 * square))
        side = 0.5 * (1.0 + bent)
        act = (pre * side).astype(BF)
        slope = side + 0.5 * pre * (1.0 - bent * bent) * (
            0.7978845608028654 * (1.0 + 0.134145 * square)
        )
        df = (right_product(dm[part].reshape(256, D), proj[...]) * slope).astype(BF)
        rows = slice(half * 256, half * 256 + 256)
        act_all[rows] = act
        df_all[rows] = df
        total += jnp.sum(df.astype(F32), axis=0, keepdims=True)
        made = plain_product(act, proj[...]).reshape(2, 128, D)
        pulled = right_product(df, fc[...]).reshape(2, 128, D)
        if half < 2:
            next_own[part] = made
            da2_own[part] = pulled
        else:
            next_other[part] = made.astype(BF)
            da2_other[part] = pulled.astype(BF)
    bias_sum[...] = jnp.broadcast_to(total, (8, 512))
    fc_sum = left_product(a2_own[...].reshape(512, D), df_all[0:512]) + left_product(
        a2_other[...].reshape(512, D), df_all[512:1024]
    )
    proj_sum = left_product(act_all[0:512], dm_own[...].reshape(512, D)) + left_product(
        act_all[512:1024], dm_other[...].reshape(512, D)
    )
    for chip in range(16):
        for side in range(2):
            row = feature_row(chip // 4, side, chip % 4)
            sums[chip, side * 32 : side * 32 + 32, :] = fc_sum[row : row + 32].astype(BF)
            sums[chip, 64 + side * 32 : 96 + side * 32, :] = proj_sum[
                chip * 32 : chip * 32 + 32, side * 512 : side * 512 + 512
            ].astype(BF)


def attended_grad_kernel(places, da, matrix, msg):
    product = right_product(da[...], matrix[...])
    turned = [pltpu.roll(product[:, i * 128 : i * 128 + 128], 64, 1) for i in range(4)]
    left = lane_half((32, 128))
    for side in range(2):
        sequence = places[3] if side == 0 else 1 - places[3]
        for part in range(2):
            for pair in range(4):
                top = side * 128 + part * 64
                bottom = top + 32
                flat = product[:, pair * 128 : pair * 128 + 128]
                msg[(sequence * 4 + part) * 4 + pair] = jnp.where(
                    left, flat[top : top + 32], turned[pair][bottom : bottom + 32]
                ).astype(BF)
                msg[(sequence * 4 + 2 + part) * 4 + pair] = jnp.where(
                    left, turned[pair][top : top + 32], flat[bottom : bottom + 32]
                ).astype(BF)


def out_grad_kernel(places, attended, da, o0, o1, o2, o3, total):
    total[...] = left_product(attended[...], da[...])
    for step, ref in enumerate((o0, o1, o2, o3)):
        z = around(places[2], step)
        ref[...] = jnp.concatenate(
            [total[pl.ds(pl.multiple_of(chip * 32 + z * 8, 8), 8), :] for chip in range(16)], axis=0
        ).astype(BF)


def input_grad_kernel(
    places, got, own, other, normed, weight, sums, dout, da_own, da_other, weight_sum, rows, dqkv, total
):
    left = lane_half((32, 128))
    for sequence in range(2):
        for head in range(2):
            task = (sequence * 2 + head) * 2
            dqkv[sequence * 512 : sequence * 512 + 512, head * 128 : head * 128 + 128] = (
                got[task, 0:512, :].astype(F32) + got[task + 1, 0:512, :].astype(F32)
            ).astype(BF)
        for part in range(2):
            for z in range(4):
                at = slice(512 + z * 32, 544 + z * 32)
                one = got[sequence * 4 + part, at, :].astype(F32)
                two = got[sequence * 4 + 2 + part, at, :].astype(F32)
                row = sequence * 512 + z * 128 + part * 64
                dqkv[row : row + 32, 256:384] = jnp.where(
                    left, one, pltpu.roll(two, 64, 1)
                ).astype(BF)
                dqkv[row + 32 : row + 64, 256:384] = jnp.where(
                    left, pltpu.roll(one, 64, 1), two
                ).astype(BF)
    column = jnp.sum(dqkv[...].astype(F32), axis=0, keepdims=True)
    column = jnp.broadcast_to(column, (8, 384))
    left8 = lane_half((8, 128))
    value_sum = jnp.where(left8, pltpu.roll(column[:, 0:128], 64, 1), column[:, 128:256])
    gain_sum = jnp.zeros((1, D), F32)
    shift_sum = jnp.zeros((1, D), F32)
    for side, source in enumerate((own, other)):
        sequence = places[3] if side == 0 else 1 - places[3]
        for step in range(4):
            z = around(places[2], step)
            begin = pl.multiple_of(sequence * 512 + z * 128, 128)
            grad = right_product(dqkv[pl.ds(begin, 128), :], weight[:, 0:384])
            values = source[step].astype(F32)
            center = values - jnp.mean(values, axis=1, keepdims=True)
            spread = jnp.mean(center * center, axis=1, keepdims=True)
            gain_sum += jnp.sum(grad * (center * lax.rsqrt(spread + EPS)), axis=0, keepdims=True)
            shift_sum += jnp.sum(grad, axis=0, keepdims=True)
            if side == 0:
                da_own[step] = grad
            else:
                da_other[step] = grad.astype(BF)
    rows[...] = sums[...]
    rows[0:1, :] = gain_sum
    rows[1:2, :] = shift_sum
    lanes = pl.ds(head_lanes(places), 128)
    rows[2:4, :] = jnp.zeros((2, D), F32)
    rows[2:3, lanes] = column[0:1, 256:384]
    rows[3:4, lanes] = value_sum[0:1]
    total[:, 0:384] = jnp.transpose(
        left_product(dqkv[...], normed[...].reshape(1024, D))
    ).astype(BF)
    total[:, 384:512] = jnp.transpose(
        jnp.concatenate([rows[...], jnp.zeros((112, D), F32)], axis=0)
    ).astype(BF)
    for chip in range(16):
        for side in range(2):
            row = feature_row(chip // 4, side, chip % 4)
            weight_sum[chip, side * 32 : side * 32 + 32, :] = total[row : row + 32, :]
        weight_sum[chip, 64:80, :] = dout[chip]


def limit_of(position, starts):
    limit = position
    for start in starts:
        limit = jnp.where((position >= start) & (position < start + PIECE), start + PIECE - 1, limit)
    return limit


def over_blocks(step, full, count, carry):
    carry = lax.fori_loop(0, full, functools.partial(step, False), carry)
    return lax.fori_loop(full, count, functools.partial(step, True), carry)


def forward_kernel(order_ref, source_ref, where_ref, starts_ref, got_ref, *refs):
    kv_ref, q_ref, o_ref, lse_ref, msg_ref, one_ref = refs[-6:]
    starts = [starts_ref[i] for i in range(6)]
    wide = lane_half((64, 128))
    left = lane_half((32, 128))

    @pl.loop(0, 8)
    def _(group):
        for i in range(8):
            stored = order_ref[group * 8 + i]
            block = got_ref[
                stored // 8, pl.ds(pl.multiple_of((stored % 8) * 64, 64), 64), :
            ]
            at = pl.ds(pl.multiple_of(group * 512 + i * 64, 64), 64)
            kv_ref[at, :] = block
            one_ref[at, :] = jnp.where(wide, jnp.ones_like(block), block)

    @pl.loop(0, 4)
    def _(group):
        for i in range(8):
            source = source_ref[group * 8 + i]
            packed = got_ref[
                source // 4, pl.ds(pl.multiple_of(512 + (source % 4) * 32, 32), 32), :
            ].astype(F32) * 0.125
            row = pl.multiple_of(group * 512 + i * 64, 64)
            q_ref[pl.ds(row, 32), :] = jnp.where(left, packed, 0.0).astype(BF)
            q_ref[pl.ds(row + 32, 32), :] = jnp.where(
                left, pltpu.roll(packed, 64, 1), 0.0
            ).astype(BF)

    @pl.loop(0, 2048 // QB)
    def _(block):
        row = pl.multiple_of(block * QB, QB)
        query = q_ref[pl.ds(row, QB), :]
        spans = QB // 64
        first = limit_of(where_ref[block * spans] * 64, starts)
        last = limit_of(where_ref[block * spans + spans - 1] * 64 + 63, starts)
        full = (first + 1) // KB
        count = last // KB + 1
        inner = lax.broadcasted_iota(jnp.int32, (64, 1), 0)
        position = jnp.concatenate(
            [where_ref[block * spans + i] * 64 + inner for i in range(spans)], axis=0
        )
        limit = limit_of(position, starts)

        def scores_of(masked, index):
            begin = pl.multiple_of(index * KB, KB)
            scores = right_product(query, kv_ref[pl.ds(begin, KB), :])
            if masked:
                key_pos = begin + lax.broadcasted_iota(jnp.int32, (1, KB), 1)
                scores = jnp.where(key_pos <= limit, scores, NEG)
            return scores

        def highest(masked, index, high):
            scores = scores_of(masked, index)
            for i in range(KB // 128):
                high = jnp.maximum(high, scores[:, i * 128 : i * 128 + 128])
            return high

        def mixture(masked, index, total):
            begin = pl.multiple_of(index * KB, KB)
            raised = jnp.exp2((scores_of(masked, index) - maxima) * LOG2E)
            return total + plain_product(raised.astype(BF), one_ref[pl.ds(begin, KB), :])

        high = over_blocks(highest, full, count, jnp.full((QB, 128), NEG, F32))
        maxima = jnp.max(high, axis=1, keepdims=True)
        total = over_blocks(mixture, full, count, jnp.zeros((QB, 128), F32))
        attended = total / pltpu.roll(total, 64, 1)
        o_ref[pl.ds(row, QB), :] = jnp.where(lane_half((QB, 128)), 0.0, attended).astype(BF)
        log_total = maxima * LOG2E + jnp.log2(total[:, 0:1])
        lse_ref[block] = jnp.transpose(jnp.broadcast_to(log_total, (QB, 128)))[0:8, :]
        turned = pltpu.roll(attended, 64, 1)
        for i in range(spans):
            top, bottom = turned[i * 64 : i * 64 + 32], attended[i * 64 + 32 : i * 64 + 64]
            msg_ref[source_ref[block * spans + i]] = jnp.where(left, top, bottom).astype(BF)


def backward_kernel(
    order_ref,
    source_ref,
    where_ref,
    starts_ref,
    kv_ref,
    q_ref,
    o_ref,
    lse_ref,
    got_ref,
    *refs,
):
    msg_ref, do_ref, sum_ref = refs[-3:]
    starts = [starts_ref[i] for i in range(6)]

    left = lane_half((32, 128))

    @pl.loop(0, 4)
    def _(group):
        for i in range(8):
            packed = got_ref[source_ref[group * 8 + i]].astype(F32)
            row = pl.multiple_of(group * 512 + i * 64, 64)
            do_ref[pl.ds(row, 32), :] = jnp.where(left, 0.0, pltpu.roll(packed, 64, 1)).astype(BF)
            do_ref[pl.ds(row + 32, 32), :] = jnp.where(left, 0.0, packed).astype(BF)

    sum_ref[...] = jnp.zeros_like(sum_ref)

    @pl.loop(0, 2048 // QB)
    def _(block):
        row = pl.multiple_of(block * QB, QB)
        query = q_ref[pl.ds(row, QB), :]
        grad = do_ref[pl.ds(row, QB), :]
        both = jnp.concatenate([query, grad], axis=0)
        spans = QB // 64
        first = limit_of(where_ref[block * spans] * 64, starts)
        last = limit_of(where_ref[block * spans + spans - 1] * 64 + 63, starts)
        full = (first + 1) // KB
        count = last // KB + 1
        inner = lax.broadcasted_iota(jnp.int32, (1, 64), 1)
        position = jnp.concatenate(
            [where_ref[block * spans + i] * 64 + inner for i in range(spans)], axis=1
        )
        limit = limit_of(position, starts)
        log_total = lse_ref[block][0:1, :]
        product = grad.astype(F32) * o_ref[pl.ds(row, QB), :].astype(F32)
        delta = lax.dot_general(
            jnp.ones((8, 128), F32),
            product,
            (((1,), (1,)), ((), ())),
            precision=lax.Precision.HIGHEST,
            preferred_element_type=F32,
        )[0:1, :]

        def step(masked, index, total):
            begin = pl.multiple_of(index * KB, KB)
            pair = kv_ref[pl.ds(begin, KB), :]
            scores = right_product(pair, query)
            if masked:
                key_pos = begin + lax.broadcasted_iota(jnp.int32, (KB, 1), 0)
                scores = jnp.where(key_pos <= limit, scores, NEG)
            weights = jnp.exp2(scores * LOG2E - log_total)
            grad_scores = (weights * (right_product(pair, grad) - delta)).astype(BF)
            sum_ref[pl.ds(begin, KB), :] += plain_product(
                jnp.concatenate([grad_scores, weights.astype(BF)], axis=1), both
            )
            return total + left_product(grad_scores, pair)

        total = over_blocks(step, full, count, jnp.zeros((QB, 128), F32)) * 0.125
        turned = pltpu.roll(total, 64, 1)
        for i in range(spans):
            top, bottom = total[i * 64 : i * 64 + 32], turned[i * 64 + 32 : i * 64 + 64]
            source = source_ref[block * spans + i]
            msg_ref[
                source // 4, pl.ds(pl.multiple_of(512 + (source % 4) * 32, 32), 32), :
            ] = jnp.where(lane_half(top.shape), top, bottom).astype(BF)

    @pl.loop(0, 8)
    def _(group):
        for i in range(8):
            stored = order_ref[group * 8 + i]
            msg_ref[stored // 8, pl.ds(pl.multiple_of((stored % 8) * 64, 64), 64), :] = sum_ref[
                pl.ds(pl.multiple_of(group * 512 + i * 64, 64), 64), :
            ].astype(BF)


def attend_forward(tables, got, after):
    shapes = [
        jax.ShapeDtypeStruct((4096, 128), BF),
        jax.ShapeDtypeStruct((2048, 128), BF),
        jax.ShapeDtypeStruct((2048, 128), BF),
        jax.ShapeDtypeStruct((2048 // QB, 8, QB), F32),
        jax.ShapeDtypeStruct((32, 32, 128), BF),
    ]
    return pl.pallas_call(
        forward_kernel,
        out_shape=shapes,
        in_specs=[pl.BlockSpec(memory_space=pltpu.SMEM)] * 4
        + [pl.BlockSpec(memory_space=pltpu.VMEM)]
        + [pl.BlockSpec(memory_space=pl.ANY)] * len(after),
        out_specs=[pl.BlockSpec(memory_space=pltpu.VMEM)] * 5,
        scratch_shapes=[pltpu.VMEM((4096, 128), BF)],
        cost_estimate=cost(25),
        compiler_params=pltpu.CompilerParams(vmem_limit_bytes=48 * 1024 * 1024),
    )(*tables, got, *after)


def attend_backward(tables, saved, got, after):
    return pl.pallas_call(
        backward_kernel,
        out_shape=jax.ShapeDtypeStruct((8, 640, 128), BF),
        in_specs=[pl.BlockSpec(memory_space=pltpu.SMEM)] * 4
        + [pl.BlockSpec(memory_space=pltpu.VMEM)] * 5
        + [pl.BlockSpec(memory_space=pl.ANY)] * len(after),
        out_specs=pl.BlockSpec(memory_space=pltpu.VMEM),
        scratch_shapes=[pltpu.VMEM((2048, 128), BF), pltpu.VMEM((4096, 128), F32)],
        cost_estimate=cost(25),
        compiler_params=pltpu.CompilerParams(vmem_limit_bytes=48 * 1024 * 1024),
    )(*tables, *saved, got, *after)


def order_tables(span_order, piece_starts, part):
    places = jnp.arange(64, dtype=jnp.int32)
    order = jnp.sum(jnp.where(span_order[None, :] == places[:, None], places[None, :], 0), axis=1)
    mine = lax.dynamic_index_in_dim(span_order.reshape(32, 2), part, 1, keepdims=False)
    rank = jnp.sum((mine[None, :] < mine[:, None]).astype(jnp.int32), axis=1)
    sources = jnp.arange(32, dtype=jnp.int32)
    hit = rank[None, :] == sources[:, None]
    source = jnp.sum(jnp.where(hit, sources[None, :], 0), axis=1)
    where = jnp.sum(jnp.where(hit, mine[None, :], 0), axis=1)
    return order.astype(jnp.int32), source.astype(jnp.int32), where.astype(jnp.int32), piece_starts


def on_device(
    tokens,
    out_grad,
    piece_starts,
    span_order,
    ln1_gain,
    ln1_bias,
    qkv_weight,
    query_bias,
    value_bias,
    out_weight,
    out_bias,
    ln2_gain,
    ln2_bias,
    fc_weight,
    fc_bias,
    proj_weight,
    proj_bias,
):
    core = lax.axis_index("core")
    z_place = lax.axis_index("z")
    x_place = lax.axis_index("x")
    y_place = lax.axis_index(Y)
    sequence = lax.axis_index("yl")
    head_part = x_place // 2
    query_part = x_place % 2
    places = jnp.stack([y_place, x_place, z_place, core]).astype(jnp.int32)
    own = tokens[0]
    dm_own = out_grad[0]

    both_tables = lax.all_gather(
        jnp.concatenate([span_order[0], piece_starts[0]]), "core", axis=0, tiled=False
    )
    table = lax.dynamic_index_in_dim(both_tables, sequence, 0, keepdims=False)
    tables = order_tables(table[:64], table[64:], query_part)

    qkv_parts = qkv_weight[0].reshape(8, 3, 2, 2, 2, 2, 64)
    kv_cols = qkv_parts[:, 1:].transpose(3, 2, 4, 0, 5, 1, 6).reshape(2, 4, 8, 256)
    q_cols = qkv_parts[:, 0].transpose(2, 1, 3, 0, 4, 5).reshape(2, 4, 8, 128)
    fc_cols = (
        fc_weight[0]
        .reshape(8, 2, 2, 2, 4, 4, 32)
        .transpose(2, 5, 0, 1, 3, 4, 6)
        .reshape(2, 4, 8, 512)
    )
    members = (
        ln1_gain,
        ln1_bias,
        query_bias,
        value_bias,
        out_bias,
        ln2_gain,
        ln2_bias,
        proj_bias,
    )
    row_index = lax.broadcasted_iota(jnp.int32, (8, 8), 0)
    vectors = jnp.zeros((8, 8), BF)
    for i, member in enumerate(members):
        vectors = jnp.where(row_index == i, member, vectors)
    vectors = jnp.concatenate(
        [
            vectors.T,
            jnp.zeros((8, 24), BF),
            jnp.pad(fc_bias, ((0, 7), (0, 0))),
            jnp.zeros((8, 64), BF),
        ],
        axis=1,
    )
    vec_cols = jnp.broadcast_to(vectors[None, None], (2, 4, 8, 128))
    packed = jnp.concatenate([kv_cols, q_cols, vec_cols, fc_cols], axis=3)
    packed = packed.reshape(8, 8, 1024)
    rows_z = ring_blocks(own, "z")
    spread = exchange(packed, ("core", "z"))


    out_rows = ring_stack(tie(out_weight[0], spread), "z")
    out_rows = jnp.roll(out_rows, z_place, axis=0).reshape(32, 2, 512)
    out_rows = out_rows.transpose(1, 0, 2).reshape(64, 512)
    first = spread_out(spread[:, :, :512].reshape(64, 512), PLANE, 16)
    proj_halves = proj_weight[0].reshape(32, 2, 512).transpose(1, 0, 2).reshape(64, 512)
    second = jnp.concatenate([spread[:, :, 512:].reshape(64, 512), proj_halves, out_rows], axis=0)
    second_x = ring_stack(second, "x")
    second = ring_blocks(second_x, Y)
    rows_z = jnp.stack(rows_z)
    rows_other = swap_core(rows_z)

    msg, normed, qkv_matrix, rows = vmem_call(
        qkv_kernel,
        [
            ((8, 640, 128), BF),
            ((2, 4, 128, D), BF),
            ((1024, 512), BF),
            ((16, D), F32),
        ],
        places,
        [first, rows_z, rows_other],
        after=[second_x],
        microseconds=5,
    )
    got = lax.all_to_all(msg, ("yl", "x"), split_axis=0, concat_axis=0, tiled=True)
    kv, query, mix, log_total, o_msg = attend_forward(
        tables, got, []
    )
    o_got = lax.all_to_all(o_msg, ("yl", "x", "z"), split_axis=0, concat_axis=0, tiled=True)
    dm_z = ring_blocks(tie(dm_own, o_msg), "z")

    out_shift, gain_two, shift_two, proj_shift = [rows[i] for i in range(4, 8)]
    part_own, part_other, o_two, out_matrix = vmem_call(
        out_kernel,
        [((128, D), F32), ((128, D), F32), ((256, 512), BF), ((512, D), BF)],
        places,
        [o_got, *second],
        after=dm_z[1:],
    )
    middle = own.astype(F32) + (part_own + swap_core(part_other) + out_shift)
    a2_own = layer_norm(middle, gain_two, shift_two).astype(BF)
    dm_z = jnp.stack(dm_z)
    dm_other = swap_core(dm_z)
    a2_z = ring_stack(a2_own, "z")
    fc_shift = qkv_matrix.reshape(2, 2, 2, 4, 4, 8, 512)[:, :, :, :, :, 0, 416:448]
    fc_shift = lax.dynamic_index_in_dim(fc_shift, core, 1, keepdims=False)
    fc_shift = lax.dynamic_index_in_dim(fc_shift, z_place, 3, keepdims=False)
    fc_shift = jnp.broadcast_to(fc_shift.reshape(1, 512).astype(F32), (8, 512))
    a2_other = swap_core(a2_z)
    next_own, next_other, da2_own, da2_other, dsecond, bias_sum = vmem_call(
        feed_kernel,
        [
            ((4, 128, D), F32),
            ((4, 128, D), BF),
            ((4, 128, D), F32),
            ((4, 128, D), BF),
            ((16, 128, 512), BF),
            ((8, 512), F32),
        ],
        places,
        [a2_z, a2_other, dm_z, dm_other, fc_shift, *second],
        [((1024, 512), BF), ((512, D), BF), ((1024, 512), BF), ((1024, 512), BF)],
        microseconds=12,
    )
    da2_got = swap_core(da2_other)
    da2 = ring_reduce([(da2_own[i] + da2_got[i].astype(F32)).astype(BF) for i in range(4)], "z")
    da2 = da2.astype(F32)
    back_two, normed_two = norm_backward(middle, gain_two, da2)
    dmid = dm_own.astype(F32) + back_two
    da_own = dmid.astype(BF)
    da_two = jnp.concatenate([da_own, swap_core(da_own)], axis=0)
    do_msg = vmem_call(
        attended_grad_kernel, [((32, 32, 128), BF)], places, [da_two, out_matrix]
    )[0]
    do_got = lax.all_to_all(do_msg, ("yl", "x", "z"), split_axis=0, concat_axis=0, tiled=True)
    next_got = swap_core(tie(next_other, do_msg))
    next_parts = [(next_own[i] + next_got[i].astype(F32)).astype(BF) for i in range(4)]
    next_sum = ring_arrive(next_parts, "z")
    final = middle + (add_all(next_sum).astype(F32) + proj_shift)
    dsecond = exchange(tie(dsecond, do_got), PLANE)
    dmsg = attend_backward(tables, (kv, query, mix, log_total), do_got, next_parts[1:])
    dout = vmem_call(
        out_grad_kernel,
        [((128, D), BF)] * 4,
        places,
        [o_two, tie(da_two, dmsg)],
        [((512, D), F32)],
    )
    dout = ring_arrive(dout, "z")
    dout = add_all(dout).reshape(16, 8, 2, 512).transpose(0, 2, 1, 3).reshape(16, 16, 512)
    dgot = exchange(tie(dmsg, dsecond, *next_sum[1:]), ("yl", "x"))

    here = (lax.broadcasted_iota(jnp.int32, (2, 4), 0) == core) & (
        lax.broadcasted_iota(jnp.int32, (2, 4), 1) == z_place
    )
    bias_rows = jnp.where(
        here[None, None, :, None, None, :, None],
        bias_sum[0].reshape(2, 2, 4, 8, 4).transpose(4, 0, 1, 2, 3)[:, :, None, :, :, None, :],
        0.0,
    ).reshape(4, 1024)
    sums = jnp.concatenate(
        [
            jnp.zeros((4, D), F32),
            jnp.stack(
                [
                    jnp.sum(da_own.astype(F32), axis=0),
                    jnp.sum(da2 * normed_two, axis=0),
                    jnp.sum(da2, axis=0),
                    jnp.sum(dm_own.astype(F32), axis=0),
                ]
            ),
            bias_rows,
            jnp.zeros((4, D), F32),
        ],
        axis=0,
    )
    da_one_own, da_one_other, dfirst = vmem_call(
        input_grad_kernel,
        [((4, 128, D), F32), ((4, 128, D), BF), ((16, 80, 512), BF)],
        places,
        [dgot, rows_z, rows_other, normed, qkv_matrix, sums, dout],
        [((16, D), F32), ((1024, 384), BF), ((1024, 512), BF)],
        microseconds=8,
    )
    dfirst = exchange(dfirst, PLANE)
    da_one_swapped = swap_core(da_one_other)
    da_one = ring_reduce(
        [(da_one_own[i] + da_one_swapped[i].astype(F32)).astype(BF) for i in range(4)], "z"
    ).astype(F32)
    dfirst = jnp.sum(dfirst.astype(F32), axis=0) + 0.0 * da_one[0, 0]
    back_one, _ = norm_backward(own.astype(F32), rows[0], da_one)
    dtokens = dmid + back_one
    dsecond = jnp.sum(dsecond.astype(F32), axis=0)
    dproj = dsecond[64:].reshape(2, 32, 512).transpose(1, 0, 2).reshape(32, D)
    grad_out = dfirst[64:].reshape(2, 8, 512).transpose(1, 0, 2).reshape(8, D)

    back = jnp.concatenate(
        [dfirst[:64].astype(BF).reshape(8, 8, 512), dsecond[:64].astype(BF).reshape(8, 8, 512)], axis=2
    )
    back = lax.all_to_all(back, ("core", "z"), split_axis=0, concat_axis=0, tiled=True).astype(F32)
    kv_back = back[:, :, :256].reshape(2, 2, 2, 8, 2, 2, 64).transpose(3, 5, 1, 0, 2, 4, 6)
    q_back = back[:, :, 256:384].reshape(2, 2, 2, 8, 2, 64).transpose(3, 1, 0, 2, 4, 5)
    grad_qkv = jnp.concatenate([q_back.reshape(8, 1024), kv_back.reshape(8, 2048)], axis=1)
    grad_fc = (
        back[:, :, 512:]
        .reshape(2, 4, 8, 2, 2, 4, 32)
        .transpose(2, 3, 0, 4, 5, 1, 6)
        .reshape(8, 4096)
    )
    totals = jnp.sum(back[:, :, 384:396], axis=0)
    vecs = [totals[:, i][None] for i in range(8)]
    return (
        final.astype(BF)[None],
        dtokens[None],
        vecs[0],
        vecs[1],
        grad_qkv[None],
        vecs[2],
        vecs[3],
        grad_out[None],
        vecs[4],
        vecs[5],
        vecs[6],
        grad_fc[None],
        totals[:, 8:].reshape(1, 32),
        dproj[None],
        vecs[7],
    )


def solution(mesh):
    fine = Mesh(mesh.devices.reshape(2, 2, 2, 4, 4), AXES)
    dp, seq, every = ("yh", "core"), ("yl", "x", "z"), AXES
    vector, matrix, tokens = P(None, every), P(None, every, None), P(dp, seq, None)
    return jax.shard_map(
        on_device,
        mesh=fine,
        in_specs=(
            tokens,
            tokens,
            P(dp, None),
            P(dp, None),
            vector,
            vector,
            matrix,
            vector,
            vector,
            matrix,
            vector,
            vector,
            vector,
            matrix,
            vector,
            matrix,
            vector,
        ),
        out_specs=(
            tokens,
            tokens,
            vector,
            vector,
            matrix,
            vector,
            vector,
            matrix,
            vector,
            vector,
            vector,
            matrix,
            vector,
            matrix,
            vector,
        ),
        check_vma=False,
    )
```

```python
import functools

import jax
import jax.numpy as jnp
from jax import lax
from jax.experimental import pallas as pl
from jax.experimental.pallas import tpu as pltpu
from jax.sharding import Mesh, PartitionSpec as P

D = 1024
PIECE = 256
EPS = 1e-05
NEG = -1e30
LOG2E = 1.4426950408889634
BF = jnp.bfloat16
F32 = jnp.float32
AXES = ("yh", "core", "yl", "x", "z")
PLANE = ("yh", "yl", "x")
Y = ("yh", "yl")
QB = 512
KB = 1024


def plain_product(left_side, right_side):
    return jnp.dot(left_side, right_side, preferred_element_type=F32)


def left_product(left_side, right_side):
    return lax.dot_general(
        left_side, right_side, (((0,), (0,)), ((), ())), preferred_element_type=F32
    )


def right_product(left_side, right_side):
    return lax.dot_general(
        left_side, right_side, (((1,), (1,)), ((), ())), preferred_element_type=F32
    )


def layer_norm(values, gain, shift):
    center = values - jnp.mean(values, axis=-1, keepdims=True)
    spread = jnp.mean(center * center, axis=-1, keepdims=True)
    return center * lax.rsqrt(spread + EPS) * gain + shift


def norm_backward(values, gain, grad):
    center = values - jnp.mean(values, axis=-1, keepdims=True)
    spread = jnp.mean(center * center, axis=-1, keepdims=True)
    scale = lax.rsqrt(spread + EPS)
    normed = center * scale
    pulled = grad * gain
    back = scale * (
        pulled
        - jnp.mean(pulled, axis=-1, keepdims=True)
        - normed * jnp.mean(pulled * normed, axis=-1, keepdims=True)
    )
    return back, normed


def shift(values, axis, step):
    return lax.ppermute(values, axis, [(i, (i + step) % 4) for i in range(4)])


def swap_core(values):
    return lax.ppermute(values, "core", [(0, 1), (1, 0)])


def ring_blocks(values, axis):
    return [values, shift(values, axis, -1), shift(values, axis, 2), shift(values, axis, 1)]


def ring_stack(values, axis):
    return jnp.stack(ring_blocks(values, axis))


def add_all(terms):
    total = terms[0].astype(F32)
    for term in terms[1:]:
        total = total + term.astype(F32)
    return total.astype(BF)


def ring_reduce(blocks, axis):
    return add_all(ring_arrive(blocks, axis))


def ring_arrive(blocks, axis):
    return [
        blocks[0],
        shift(blocks[1], axis, 1),
        shift(blocks[2], axis, 2),
        shift(blocks[3], axis, -1),
    ]


def exchange(values, axes):
    return lax.all_to_all(values, axes, split_axis=0, concat_axis=0, tiled=True)


def spread_out(values, axes, count):
    return exchange(jnp.broadcast_to(values[None], (count,) + values.shape), axes)


def around(place, step):
    return lax.rem(place + step, 4)


def feature_row(y, side, x):
    return (y // 2) * 512 + side * 256 + (y % 2) * 128 + x * 32


def cost(microseconds):
    return pl.CostEstimate(
        flops=microseconds * 1_000_000_000, bytes_accessed=1, transcendentals=0
    )


def vmem_call(kernel, out_shape, places, arrays, scratch=(), after=(), microseconds=2):
    count = len(arrays)

    def body(*refs):
        kernel(*refs[: 1 + count], *refs[1 + count + len(after) :])

    return pl.pallas_call(
        body,
        out_shape=[jax.ShapeDtypeStruct(shape, dtype) for shape, dtype in out_shape],
        in_specs=[pl.BlockSpec(memory_space=pltpu.SMEM)]
        + [pl.BlockSpec(memory_space=pltpu.VMEM)] * count
        + [pl.BlockSpec(memory_space=pl.ANY)] * len(after),
        out_specs=[pl.BlockSpec(memory_space=pltpu.VMEM)] * len(out_shape),
        scratch_shapes=[pltpu.VMEM(shape, dtype) for shape, dtype in scratch],
        cost_estimate=cost(microseconds),
        compiler_params=pltpu.CompilerParams(vmem_limit_bytes=50 * 1024 * 1024),
    )(places, *arrays, *after)


def tie_kernel(*refs):
    pass


def tie(values, *after):
    return pl.pallas_call(
        tie_kernel,
        out_shape=jax.ShapeDtypeStruct(values.shape, values.dtype),
        in_specs=[pl.BlockSpec(memory_space=pl.ANY)] * (1 + len(after)),
        out_specs=pl.BlockSpec(memory_space=pl.ANY),
        input_output_aliases={0: 0},
    )(values, *after)


def lane_half(shape):
    return lax.broadcasted_iota(jnp.int32, shape, 1) < 64


def head_lanes(places):
    z, core = places[2], places[3]
    return pl.multiple_of((z // 2) * 512 + core * 256 + (z % 2) * 128, 128)


def qkv_kernel(places, source_weight, own, other, msg, normed, weight, rows):
    for chip in range(16):
        for side in range(2):
            row = feature_row(chip // 4, side, chip % 4)
            weight[row : row + 32, :] = source_weight[chip, side * 32 : side * 32 + 32, :]
    vectors = weight[:, 384:512].astype(F32)
    rows[...] = jnp.transpose(vectors)[0:16, :]
    gain, shift_row = rows[0:1, :], rows[1:2, :]
    lanes = pl.ds(head_lanes(places), 128)
    query_add = rows[2:3, lanes]
    value_add = jnp.broadcast_to(rows[3:4, lanes], (8, 128))
    left8 = lane_half((8, 128))
    first_add = jnp.where(left8, 0.0, pltpu.roll(value_add, 64, 1))[0:1]
    second_add = jnp.where(left8, 0.0, value_add)[0:1]
    left = lane_half((32, 128))
    for side, source in enumerate((own, other)):
        sequence = places[3] if side == 0 else 1 - places[3]
        for step in range(4):
            z = around(places[2], step)
            values = source[step].astype(F32)
            center = values - jnp.mean(values, axis=1, keepdims=True)
            spread = jnp.mean(center * center, axis=1, keepdims=True)
            row = (center * lax.rsqrt(spread + EPS) * gain + shift_row).astype(BF)
            normed[sequence, z] = row
            made = plain_product(row, weight[:, 0:384])
            pairs = (
                (made[:, 0:128] + first_add).astype(BF),
                (made[:, 128:256] + second_add).astype(BF),
            )
            query = made[:, 256:384] + query_add
            turned = pltpu.roll(query, 64, 1)
            begin = pl.multiple_of(z * 128, 128)
            q_begin = pl.multiple_of(512 + z * 32, 32)
            for part in range(2):
                top, bottom = part * 64, part * 64 + 32
                packed = (
                    jnp.where(left, query[top : top + 32], turned[bottom : bottom + 32]),
                    jnp.where(left, turned[top : top + 32], query[bottom : bottom + 32]),
                )
                for head in range(2):
                    task = sequence * 4 + head * 2 + part
                    msg[task, pl.ds(begin, 128), :] = pairs[head]
                    msg[task, pl.ds(q_begin, 32), :] = packed[head].astype(BF)


def out_kernel(places, got, b0, b1, b2, b3, own, other, attended, matrix):
    for up, ref in enumerate((b0, b1, b2, b3)):
        y = around(places[0], up)
        for turn in range(4):
            x = around(places[1], turn)
            row = pl.ds(pl.multiple_of((y * 4 + x) * 32, 32), 32)
            matrix[row, 0:512] = ref[turn, 128:160, :]
            matrix[row, 512:1024] = ref[turn, 160:192, :]
    left = lane_half((32, 128))
    for side in range(2):
        sequence = places[3] if side == 0 else 1 - places[3]
        for part in range(2):
            for pair in range(4):
                one = got[(sequence * 4 + part) * 4 + pair].astype(F32)
                two = got[(sequence * 4 + 2 + part) * 4 + pair].astype(F32)
                row = side * 128 + part * 64
                columns = slice(pair * 128, pair * 128 + 128)
                attended[row : row + 32, columns] = jnp.where(
                    left, one, pltpu.roll(two, 64, 1)
                ).astype(BF)
                attended[row + 32 : row + 64, columns] = jnp.where(
                    left, pltpu.roll(one, 64, 1), two
                ).astype(BF)
    product = plain_product(attended[...], matrix[...])
    own[...] = product[0:128]
    other[...] = product[128:256]


def feed_kernel(
    places,
    a2_own,
    a2_other,
    dm_own,
    dm_other,
    bias,
    w0,
    w1,
    w2,
    w3,
    next_own,
    next_other,
    da2_own,
    da2_other,
    sums,
    bias_sum,
    fc,
    proj,
    act_all,
    df_all,
):
    for up, weights in enumerate((w0, w1, w2, w3)):
        y = around(places[0], up)
        for turn in range(4):
            x = around(places[1], turn)
            for side in range(2):
                fc[pl.ds(pl.multiple_of(feature_row(y, side, x), 32), 32), :] = weights[
                    turn, side * 32 : side * 32 + 32, :
                ]
                proj[
                    pl.ds(pl.multiple_of((y * 4 + x) * 32, 32), 32),
                    side * 512 : side * 512 + 512,
                ] = weights[turn, 64 + side * 32 : 96 + side * 32, :]
    total = jnp.zeros((1, 512), F32)
    for half in range(4):
        a2, dm = (a2_own, dm_own) if half < 2 else (a2_other, dm_other)
        part = slice(half % 2 * 2, half % 2 * 2 + 2)
        pre = plain_product(a2[part].reshape(256, D), fc[...]) + bias[0:1, :]
        square = pre * pre
        bent = jnp.tanh(0.7978845608028654 * pre * (1.0 + 0.044715 * square))
        side = 0.5 * (1.0 + bent)
        act = (pre * side).astype(BF)
        slope = side + 0.5 * pre * (1.0 - bent * bent) * (
            0.7978845608028654 * (1.0 + 0.134145 * square)
        )
        df = (right_product(dm[part].reshape(256, D), proj[...]) * slope).astype(BF)
        rows = slice(half * 256, half * 256 + 256)
        act_all[rows] = act
        df_all[rows] = df
        total += jnp.sum(df.astype(F32), axis=0, keepdims=True)
        made = plain_product(act, proj[...]).reshape(2, 128, D)
        pulled = right_product(df, fc[...]).reshape(2, 128, D)
        if half < 2:
            next_own[part] = made
            da2_own[part] = pulled
        else:
            next_other[part] = made.astype(BF)
            da2_other[part] = pulled.astype(BF)
    bias_sum[...] = jnp.broadcast_to(total, (8, 512))
    fc_sum = left_product(a2_own[...].reshape(512, D), df_all[0:512]) + left_product(
        a2_other[...].reshape(512, D), df_all[512:1024]
    )
    proj_sum = left_product(act_all[0:512], dm_own[...].reshape(512, D)) + left_product(
        act_all[512:1024], dm_other[...].reshape(512, D)
    )
    for chip in range(16):
        for side in range(2):
            row = feature_row(chip // 4, side, chip % 4)
            sums[chip, side * 32 : side * 32 + 32, :] = fc_sum[row : row + 32].astype(BF)
            sums[chip, 64 + side * 32 : 96 + side * 32, :] = proj_sum[
                chip * 32 : chip * 32 + 32, side * 512 : side * 512 + 512
            ].astype(BF)


def attended_grad_kernel(places, da, matrix, msg):
    product = right_product(da[...], matrix[...])
    turned = [pltpu.roll(product[:, i * 128 : i * 128 + 128], 64, 1) for i in range(4)]
    left = lane_half((32, 128))
    for side in range(2):
        sequence = places[3] if side == 0 else 1 - places[3]
        for part in range(2):
            for pair in range(4):
                top = side * 128 + part * 64
                bottom = top + 32
                flat = product[:, pair * 128 : pair * 128 + 128]
                msg[(sequence * 4 + part) * 4 + pair] = jnp.where(
                    left, flat[top : top + 32], turned[pair][bottom : bottom + 32]
                ).astype(BF)
                msg[(sequence * 4 + 2 + part) * 4 + pair] = jnp.where(
                    left, turned[pair][top : top + 32], flat[bottom : bottom + 32]
                ).astype(BF)


def out_grad_kernel(places, attended, da, o0, o1, o2, o3, total):
    total[...] = left_product(attended[...], da[...])
    for step, ref in enumerate((o0, o1, o2, o3)):
        z = around(places[2], step)
        ref[...] = jnp.concatenate(
            [total[pl.ds(pl.multiple_of(chip * 32 + z * 8, 8), 8), :] for chip in range(16)], axis=0
        ).astype(BF)


def input_grad_kernel(
    places, got, own, other, normed, weight, sums, dout, da_own, da_other, weight_sum, rows, dqkv, total
):
    left = lane_half((32, 128))
    for sequence in range(2):
        for head in range(2):
            task = (sequence * 2 + head) * 2
            dqkv[sequence * 512 : sequence * 512 + 512, head * 128 : head * 128 + 128] = (
                got[task, 0:512, :].astype(F32) + got[task + 1, 0:512, :].astype(F32)
            ).astype(BF)
        for part in range(2):
            for z in range(4):
                at = slice(512 + z * 32, 544 + z * 32)
                one = got[sequence * 4 + part, at, :].astype(F32)
                two = got[sequence * 4 + 2 + part, at, :].astype(F32)
                row = sequence * 512 + z * 128 + part * 64
                dqkv[row : row + 32, 256:384] = jnp.where(
                    left, one, pltpu.roll(two, 64, 1)
                ).astype(BF)
                dqkv[row + 32 : row + 64, 256:384] = jnp.where(
                    left, pltpu.roll(one, 64, 1), two
                ).astype(BF)
    column = jnp.sum(dqkv[...].astype(F32), axis=0, keepdims=True)
    column = jnp.broadcast_to(column, (8, 384))
    left8 = lane_half((8, 128))
    value_sum = jnp.where(left8, pltpu.roll(column[:, 0:128], 64, 1), column[:, 128:256])
    gain_sum = jnp.zeros((1, D), F32)
    shift_sum = jnp.zeros((1, D), F32)
    for side, source in enumerate((own, other)):
        sequence = places[3] if side == 0 else 1 - places[3]
        for step in range(4):
            z = around(places[2], step)
            begin = pl.multiple_of(sequence * 512 + z * 128, 128)
            grad = right_product(dqkv[pl.ds(begin, 128), :], weight[:, 0:384])
            values = source[step].astype(F32)
            center = values - jnp.mean(values, axis=1, keepdims=True)
            spread = jnp.mean(center * center, axis=1, keepdims=True)
            gain_sum += jnp.sum(grad * (center * lax.rsqrt(spread + EPS)), axis=0, keepdims=True)
            shift_sum += jnp.sum(grad, axis=0, keepdims=True)
            if side == 0:
                da_own[step] = grad
            else:
                da_other[step] = grad.astype(BF)
    rows[...] = sums[...]
    rows[0:1, :] = gain_sum
    rows[1:2, :] = shift_sum
    lanes = pl.ds(head_lanes(places), 128)
    rows[2:4, :] = jnp.zeros((2, D), F32)
    rows[2:3, lanes] = column[0:1, 256:384]
    rows[3:4, lanes] = value_sum[0:1]
    total[:, 0:384] = jnp.transpose(
        left_product(dqkv[...], normed[...].reshape(1024, D))
    ).astype(BF)
    total[:, 384:512] = jnp.transpose(
        jnp.concatenate([rows[...], jnp.zeros((112, D), F32)], axis=0)
    ).astype(BF)
    for chip in range(16):
        for side in range(2):
            row = feature_row(chip // 4, side, chip % 4)
            weight_sum[chip, side * 32 : side * 32 + 32, :] = total[row : row + 32, :]
        weight_sum[chip, 64:80, :] = dout[chip]


def limit_of(position, starts):
    limit = position
    for start in starts:
        limit = jnp.where((position >= start) & (position < start + PIECE), start + PIECE - 1, limit)
    return limit


def over_blocks(step, full, count, carry):
    carry = lax.fori_loop(0, full, functools.partial(step, False), carry)
    return lax.fori_loop(full, count, functools.partial(step, True), carry)


def forward_kernel(order_ref, source_ref, where_ref, starts_ref, got_ref, *refs):
    kv_ref, q_ref, o_ref, lse_ref, msg_ref, one_ref = refs[-6:]
    starts = [starts_ref[i] for i in range(6)]
    wide = lane_half((64, 128))
    left = lane_half((32, 128))

    @pl.loop(0, 8)
    def _(group):
        for i in range(8):
            stored = order_ref[group * 8 + i]
            block = got_ref[
                stored // 8, pl.ds(pl.multiple_of((stored % 8) * 64, 64), 64), :
            ]
            at = pl.ds(pl.multiple_of(group * 512 + i * 64, 64), 64)
            kv_ref[at, :] = block
            one_ref[at, :] = jnp.where(wide, jnp.ones_like(block), block)

    @pl.loop(0, 4)
    def _(group):
        for i in range(8):
            source = source_ref[group * 8 + i]
            packed = got_ref[
                source // 4, pl.ds(pl.multiple_of(512 + (source % 4) * 32, 32), 32), :
            ].astype(F32) * 0.125
            row = pl.multiple_of(group * 512 + i * 64, 64)
            q_ref[pl.ds(row, 32), :] = jnp.where(left, packed, 0.0).astype(BF)
            q_ref[pl.ds(row + 32, 32), :] = jnp.where(
                left, pltpu.roll(packed, 64, 1), 0.0
            ).astype(BF)

    @pl.loop(0, 2048 // QB)
    def _(block):
        row = pl.multiple_of(block * QB, QB)
        query = q_ref[pl.ds(row, QB), :]
        spans = QB // 64
        first = limit_of(where_ref[block * spans] * 64, starts)
        last = limit_of(where_ref[block * spans + spans - 1] * 64 + 63, starts)
        full = (first + 1) // KB
        count = last // KB + 1
        inner = lax.broadcasted_iota(jnp.int32, (64, 1), 0)
        position = jnp.concatenate(
            [where_ref[block * spans + i] * 64 + inner for i in range(spans)], axis=0
        )
        limit = limit_of(position, starts)

        def scores_of(masked, index):
            begin = pl.multiple_of(index * KB, KB)
            scores = right_product(query, kv_ref[pl.ds(begin, KB), :])
            if masked:
                key_pos = begin + lax.broadcasted_iota(jnp.int32, (1, KB), 1)
                scores = jnp.where(key_pos <= limit, scores, NEG)
            return scores

        def highest(masked, index, high):
            scores = scores_of(masked, index)
            for i in range(KB // 128):
                high = jnp.maximum(high, scores[:, i * 128 : i * 128 + 128])
            return high

        def mixture(masked, index, total):
            begin = pl.multiple_of(index * KB, KB)
            raised = jnp.exp2((scores_of(masked, index) - maxima) * LOG2E)
            return total + plain_product(raised.astype(BF), one_ref[pl.ds(begin, KB), :])

        high = over_blocks(highest, full, count, jnp.full((QB, 128), NEG, F32))
        maxima = jnp.max(high, axis=1, keepdims=True)
        total = over_blocks(mixture, full, count, jnp.zeros((QB, 128), F32))
        attended = total / pltpu.roll(total, 64, 1)
        o_ref[pl.ds(row, QB), :] = jnp.where(lane_half((QB, 128)), 0.0, attended).astype(BF)
        log_total = maxima * LOG2E + jnp.log2(total[:, 0:1])
        lse_ref[block] = jnp.transpose(jnp.broadcast_to(log_total, (QB, 128)))[0:8, :]
        turned = pltpu.roll(attended, 64, 1)
        for i in range(spans):
            top, bottom = turned[i * 64 : i * 64 + 32], attended[i * 64 + 32 : i * 64 + 64]
            msg_ref[source_ref[block * spans + i]] = jnp.where(left, top, bottom).astype(BF)


def backward_kernel(
    order_ref,
    source_ref,
    where_ref,
    starts_ref,
    kv_ref,
    q_ref,
    o_ref,
    lse_ref,
    got_ref,
    *refs,
):
    msg_ref, do_ref, sum_ref = refs[-3:]
    starts = [starts_ref[i] for i in range(6)]

    left = lane_half((32, 128))

    @pl.loop(0, 4)
    def _(group):
        for i in range(8):
            packed = got_ref[source_ref[group * 8 + i]].astype(F32)
            row = pl.multiple_of(group * 512 + i * 64, 64)
            do_ref[pl.ds(row, 32), :] = jnp.where(left, 0.0, pltpu.roll(packed, 64, 1)).astype(BF)
            do_ref[pl.ds(row + 32, 32), :] = jnp.where(left, 0.0, packed).astype(BF)

    sum_ref[...] = jnp.zeros_like(sum_ref)

    @pl.loop(0, 2048 // QB)
    def _(block):
        row = pl.multiple_of(block * QB, QB)
        query = q_ref[pl.ds(row, QB), :]
        grad = do_ref[pl.ds(row, QB), :]
        both = jnp.concatenate([query, grad], axis=0)
        spans = QB // 64
        first = limit_of(where_ref[block * spans] * 64, starts)
        last = limit_of(where_ref[block * spans + spans - 1] * 64 + 63, starts)
        full = (first + 1) // KB
        count = last // KB + 1
        inner = lax.broadcasted_iota(jnp.int32, (1, 64), 1)
        position = jnp.concatenate(
            [where_ref[block * spans + i] * 64 + inner for i in range(spans)], axis=1
        )
        limit = limit_of(position, starts)
        log_total = lse_ref[block][0:1, :]
        product = grad.astype(F32) * o_ref[pl.ds(row, QB), :].astype(F32)
        delta = lax.dot_general(
            jnp.ones((8, 128), F32),
            product,
            (((1,), (1,)), ((), ())),
            precision=lax.Precision.HIGHEST,
            preferred_element_type=F32,
        )[0:1, :]

        def step(masked, index, total):
            begin = pl.multiple_of(index * KB, KB)
            pair = kv_ref[pl.ds(begin, KB), :]
            scores = right_product(pair, query)
            if masked:
                key_pos = begin + lax.broadcasted_iota(jnp.int32, (KB, 1), 0)
                scores = jnp.where(key_pos <= limit, scores, NEG)
            weights = jnp.exp2(scores * LOG2E - log_total)
            grad_scores = (weights * (right_product(pair, grad) - delta)).astype(BF)
            sum_ref[pl.ds(begin, KB), :] += plain_product(
                jnp.concatenate([grad_scores, weights.astype(BF)], axis=1), both
            )
            return total + left_product(grad_scores, pair)

        total = over_blocks(step, full, count, jnp.zeros((QB, 128), F32)) * 0.125
        turned = pltpu.roll(total, 64, 1)
        for i in range(spans):
            top, bottom = total[i * 64 : i * 64 + 32], turned[i * 64 + 32 : i * 64 + 64]
            source = source_ref[block * spans + i]
            msg_ref[
                source // 4, pl.ds(pl.multiple_of(512 + (source % 4) * 32, 32), 32), :
            ] = jnp.where(lane_half(top.shape), top, bottom).astype(BF)

    @pl.loop(0, 8)
    def _(group):
        for i in range(8):
            stored = order_ref[group * 8 + i]
            msg_ref[stored // 8, pl.ds(pl.multiple_of((stored % 8) * 64, 64), 64), :] = sum_ref[
                pl.ds(pl.multiple_of(group * 512 + i * 64, 64), 64), :
            ].astype(BF)


def attend_forward(tables, got, after):
    shapes = [
        jax.ShapeDtypeStruct((4096, 128), BF),
        jax.ShapeDtypeStruct((2048, 128), BF),
        jax.ShapeDtypeStruct((2048, 128), BF),
        jax.ShapeDtypeStruct((2048 // QB, 8, QB), F32),
        jax.ShapeDtypeStruct((32, 32, 128), BF),
    ]
    return pl.pallas_call(
        forward_kernel,
        out_shape=shapes,
        in_specs=[pl.BlockSpec(memory_space=pltpu.SMEM)] * 4
        + [pl.BlockSpec(memory_space=pltpu.VMEM)]
        + [pl.BlockSpec(memory_space=pl.ANY)] * len(after),
        out_specs=[pl.BlockSpec(memory_space=pltpu.VMEM)] * 5,
        scratch_shapes=[pltpu.VMEM((4096, 128), BF)],
        cost_estimate=cost(25),
        compiler_params=pltpu.CompilerParams(vmem_limit_bytes=48 * 1024 * 1024),
    )(*tables, got, *after)


def attend_backward(tables, saved, got, after):
    return pl.pallas_call(
        backward_kernel,
        out_shape=jax.ShapeDtypeStruct((8, 640, 128), BF),
        in_specs=[pl.BlockSpec(memory_space=pltpu.SMEM)] * 4
        + [pl.BlockSpec(memory_space=pltpu.VMEM)] * 5
        + [pl.BlockSpec(memory_space=pl.ANY)] * len(after),
        out_specs=pl.BlockSpec(memory_space=pltpu.VMEM),
        scratch_shapes=[pltpu.VMEM((2048, 128), BF), pltpu.VMEM((4096, 128), F32)],
        cost_estimate=cost(25),
        compiler_params=pltpu.CompilerParams(vmem_limit_bytes=48 * 1024 * 1024),
    )(*tables, *saved, got, *after)


def order_tables(span_order, piece_starts, part):
    places = jnp.arange(64, dtype=jnp.int32)
    order = jnp.sum(jnp.where(span_order[None, :] == places[:, None], places[None, :], 0), axis=1)
    mine = lax.dynamic_index_in_dim(span_order.reshape(32, 2), part, 1, keepdims=False)
    rank = jnp.sum((mine[None, :] < mine[:, None]).astype(jnp.int32), axis=1)
    sources = jnp.arange(32, dtype=jnp.int32)
    hit = rank[None, :] == sources[:, None]
    source = jnp.sum(jnp.where(hit, sources[None, :], 0), axis=1)
    where = jnp.sum(jnp.where(hit, mine[None, :], 0), axis=1)
    return order.astype(jnp.int32), source.astype(jnp.int32), where.astype(jnp.int32), piece_starts


def on_device(
    tokens,
    out_grad,
    piece_starts,
    span_order,
    ln1_gain,
    ln1_bias,
    qkv_weight,
    query_bias,
    value_bias,
    out_weight,
    out_bias,
    ln2_gain,
    ln2_bias,
    fc_weight,
    fc_bias,
    proj_weight,
    proj_bias,
):
    core = lax.axis_index("core")
    z_place = lax.axis_index("z")
    x_place = lax.axis_index("x")
    y_place = lax.axis_index(Y)
    sequence = lax.axis_index("yl")
    head_part = x_place // 2
    query_part = x_place % 2
    places = jnp.stack([y_place, x_place, z_place, core]).astype(jnp.int32)
    own = tokens[0]
    dm_own = out_grad[0]

    both_tables = lax.all_gather(
        jnp.concatenate([span_order[0], piece_starts[0]]), "core", axis=0, tiled=False
    )
    table = lax.dynamic_index_in_dim(both_tables, sequence, 0, keepdims=False)
    tables = order_tables(table[:64], table[64:], query_part)

    qkv_parts = qkv_weight[0].reshape(8, 3, 2, 2, 2, 2, 64)
    kv_cols = qkv_parts[:, 1:].transpose(3, 2, 4, 0, 5, 1, 6).reshape(2, 4, 8, 256)
    q_cols = qkv_parts[:, 0].transpose(2, 1, 3, 0, 4, 5).reshape(2, 4, 8, 128)
    fc_cols = (
        fc_weight[0]
        .reshape(8, 2, 2, 2, 4, 4, 32)
        .transpose(2, 5, 0, 1, 3, 4, 6)
        .reshape(2, 4, 8, 512)
    )
    members = (
        ln1_gain,
        ln1_bias,
        query_bias,
        value_bias,
        out_bias,
        ln2_gain,
        ln2_bias,
        proj_bias,
    )
    row_index = lax.broadcasted_iota(jnp.int32, (8, 8), 0)
    vectors = jnp.zeros((8, 8), BF)
    for i, member in enumerate(members):
        vectors = jnp.where(row_index == i, member, vectors)
    vectors = jnp.concatenate(
        [
            vectors.T,
            jnp.zeros((8, 24), BF),
            jnp.pad(fc_bias, ((0, 7), (0, 0))),
            jnp.zeros((8, 64), BF),
        ],
        axis=1,
    )
    vec_cols = jnp.broadcast_to(vectors[None, None], (2, 4, 8, 128))
    packed = jnp.concatenate([kv_cols, q_cols, vec_cols, fc_cols], axis=3)
    packed = packed.reshape(8, 8, 1024)
    rows_z = ring_blocks(own, "z")
    spread = exchange(packed, ("core", "z"))


    out_rows = ring_stack(tie(out_weight[0], spread), "z")
    out_rows = jnp.roll(out_rows, z_place, axis=0).reshape(32, 2, 512)
    out_rows = out_rows.transpose(1, 0, 2).reshape(64, 512)
    first = spread_out(spread[:, :, :512].reshape(64, 512), PLANE, 16)
    proj_halves = proj_weight[0].reshape(32, 2, 512).transpose(1, 0, 2).reshape(64, 512)
    second = jnp.concatenate([spread[:, :, 512:].reshape(64, 512), proj_halves, out_rows], axis=0)
    second_x = ring_stack(second, "x")
    second = ring_blocks(second_x, Y)
    rows_z = jnp.stack(rows_z)
    rows_other = swap_core(rows_z)

    msg, normed, qkv_matrix, rows = vmem_call(
        qkv_kernel,
        [
            ((8, 640, 128), BF),
            ((2, 4, 128, D), BF),
            ((1024, 512), BF),
            ((16, D), F32),
        ],
        places,
        [first, rows_z, rows_other],
        after=[second_x],
        microseconds=5,
    )
    got = lax.all_to_all(msg, ("yl", "x"), split_axis=0, concat_axis=0, tiled=True)
    kv, query, mix, log_total, o_msg = attend_forward(
        tables, got, []
    )
    o_got = lax.all_to_all(o_msg, ("yl", "x", "z"), split_axis=0, concat_axis=0, tiled=True)
    dm_z = ring_blocks(tie(dm_own, o_msg), "z")

    out_shift, gain_two, shift_two, proj_shift = [rows[i] for i in range(4, 8)]
    part_own, part_other, o_two, out_matrix = vmem_call(
        out_kernel,
        [((128, D), F32), ((128, D), F32), ((256, 512), BF), ((512, D), BF)],
        places,
        [o_got, *second],
        after=dm_z[1:],
    )
    middle = own.astype(F32) + (part_own + swap_core(part_other) + out_shift)
    a2_own = layer_norm(middle, gain_two, shift_two).astype(BF)
    dm_z = jnp.stack(dm_z)
    dm_other = swap_core(dm_z)
    a2_z = ring_stack(a2_own, "z")
    fc_shift = qkv_matrix.reshape(2, 2, 2, 4, 4, 8, 512)[:, :, :, :, :, 0, 416:448]
    fc_shift = lax.dynamic_index_in_dim(fc_shift, core, 1, keepdims=False)
    fc_shift = lax.dynamic_index_in_dim(fc_shift, z_place, 3, keepdims=False)
    fc_shift = jnp.broadcast_to(fc_shift.reshape(1, 512).astype(F32), (8, 512))
    a2_other = swap_core(a2_z)
    next_own, next_other, da2_own, da2_other, dsecond, bias_sum = vmem_call(
        feed_kernel,
        [
            ((4, 128, D), F32),
            ((4, 128, D), BF),
            ((4, 128, D), F32),
            ((4, 128, D), BF),
            ((16, 128, 512), BF),
            ((8, 512), F32),
        ],
        places,
        [a2_z, a2_other, dm_z, dm_other, fc_shift, *second],
        [((1024, 512), BF), ((512, D), BF), ((1024, 512), BF), ((1024, 512), BF)],
        microseconds=12,
    )
    da2_got = swap_core(da2_other)
    da2 = ring_reduce([(da2_own[i] + da2_got[i].astype(F32)).astype(BF) for i in range(4)], "z")
    da2 = da2.astype(F32)
    back_two, normed_two = norm_backward(middle, gain_two, da2)
    dmid = dm_own.astype(F32) + back_two
    da_own = dmid.astype(BF)
    da_two = jnp.concatenate([da_own, swap_core(da_own)], axis=0)
    do_msg = vmem_call(
        attended_grad_kernel, [((32, 32, 128), BF)], places, [da_two, out_matrix]
    )[0]
    do_got = lax.all_to_all(do_msg, ("yl", "x", "z"), split_axis=0, concat_axis=0, tiled=True)
    next_got = swap_core(tie(next_other, do_msg))
    next_parts = [(next_own[i] + next_got[i].astype(F32)).astype(BF) for i in range(4)]
    next_sum = ring_arrive(next_parts, "z")
    final = middle + (add_all(next_sum).astype(F32) + proj_shift)
    dsecond = exchange(tie(dsecond, do_got), PLANE)
    dmsg = attend_backward(tables, (kv, query, mix, log_total), do_got, next_parts[1:])
    dout = vmem_call(
        out_grad_kernel,
        [((128, D), BF)] * 4,
        places,
        [o_two, tie(da_two, dmsg)],
        [((512, D), F32)],
    )
    dout = ring_arrive(dout, "z")
    dout = add_all(dout).reshape(16, 8, 2, 512).transpose(0, 2, 1, 3).reshape(16, 16, 512)
    dgot = exchange(tie(dmsg, dsecond, *next_sum[1:]), ("yl", "x"))

    here = (lax.broadcasted_iota(jnp.int32, (2, 4), 0) == core) & (
        lax.broadcasted_iota(jnp.int32, (2, 4), 1) == z_place
    )
    bias_rows = jnp.where(
        here[None, None, :, None, None, :, None],
        bias_sum[0].reshape(2, 2, 4, 8, 4).transpose(4, 0, 1, 2, 3)[:, :, None, :, :, None, :],
        0.0,
    ).reshape(4, 1024)
    sums = jnp.concatenate(
        [
            jnp.zeros((4, D), F32),
            jnp.stack(
                [
                    jnp.sum(da_own.astype(F32), axis=0),
                    jnp.sum(da2 * normed_two, axis=0),
                    jnp.sum(da2, axis=0),
                    jnp.sum(dm_own.astype(F32), axis=0),
                ]
            ),
            bias_rows,
            jnp.zeros((4, D), F32),
        ],
        axis=0,
    )
    da_one_own, da_one_other, dfirst = vmem_call(
        input_grad_kernel,
        [((4, 128, D), F32), ((4, 128, D), BF), ((16, 80, 512), BF)],
        places,
        [dgot, rows_z, rows_other, normed, qkv_matrix, sums, dout],
        [((16, D), F32), ((1024, 384), BF), ((1024, 512), BF)],
        microseconds=8,
    )
    dfirst = exchange(dfirst, PLANE)
    da_one_swapped = swap_core(da_one_other)
    da_one = ring_reduce(
        [(da_one_own[i] + da_one_swapped[i].astype(F32)).astype(BF) for i in range(4)], "z"
    ).astype(F32)
    dfirst = jnp.sum(dfirst.astype(F32), axis=0) + 0.0 * da_one[0, 0]
    dsecond = jnp.sum(dsecond.astype(F32), axis=0)
    dproj = dsecond[64:].reshape(2, 32, 512).transpose(1, 0, 2).reshape(32, D)
    grad_out = dfirst[64:].reshape(2, 8, 512).transpose(1, 0, 2).reshape(8, D)

    back = jnp.concatenate(
        [dfirst[:64].astype(BF).reshape(8, 8, 512), dsecond[:64].astype(BF).reshape(8, 8, 512)], axis=2
    )
    back_one, _ = norm_backward(own.astype(F32), rows[0], tie(da_one, back))
    dtokens = dmid + back_one
    back = lax.all_to_all(back, ("core", "z"), split_axis=0, concat_axis=0, tiled=True).astype(F32)
    kv_back = back[:, :, :256].reshape(2, 2, 2, 8, 2, 2, 64).transpose(3, 5, 1, 0, 2, 4, 6)
    q_back = back[:, :, 256:384].reshape(2, 2, 2, 8, 2, 64).transpose(3, 1, 0, 2, 4, 5)
    grad_qkv = jnp.concatenate([q_back.reshape(8, 1024), kv_back.reshape(8, 2048)], axis=1)
    grad_fc = (
        back[:, :, 512:]
        .reshape(2, 4, 8, 2, 2, 4, 32)
        .transpose(2, 3, 0, 4, 5, 1, 6)
        .reshape(8, 4096)
    )
    totals = jnp.sum(back[:, :, 384:396], axis=0)
    vecs = [totals[:, i][None] for i in range(8)]
    return (
        final.astype(BF)[None],
        dtokens[None],
        vecs[0],
        vecs[1],
        grad_qkv[None],
        vecs[2],
        vecs[3],
        grad_out[None],
        vecs[4],
        vecs[5],
        vecs[6],
        grad_fc[None],
        totals[:, 8:].reshape(1, 32),
        dproj[None],
        vecs[7],
    )


def solution(mesh):
    fine = Mesh(mesh.devices.reshape(2, 2, 2, 4, 4), AXES)
    dp, seq, every = ("yh", "core"), ("yl", "x", "z"), AXES
    vector, matrix, tokens = P(None, every), P(None, every, None), P(dp, seq, None)
    return jax.shard_map(
        on_device,
        mesh=fine,
        in_specs=(
            tokens,
            tokens,
            P(dp, None),
            P(dp, None),
            vector,
            vector,
            matrix,
            vector,
            vector,
            matrix,
            vector,
            vector,
            vector,
            matrix,
            vector,
            matrix,
            vector,
        ),
        out_specs=(
            tokens,
            tokens,
            vector,
            vector,
            matrix,
            vector,
            vector,
            matrix,
            vector,
            vector,
            vector,
            matrix,
            vector,
            matrix,
            vector,
        ),
        check_vma=False,
    )
```
